256 devices in a mesh: sub: 8 (over y, core), region: 32 (over z, x).
Axes of the slice: x: 4, y: 4, z: 8, core: 2. Of those that a mesh axis runs over, the one named last changes fastest.
Arguments:
- pieces: float32 [64, 32, 32, 512], P('sub', 'region'), may hold values from -6 to 6
- local_inverse: float32 [64, 32, 512, 512], P('sub', 'region'), may hold values from -0.25 to 0.25
- primal_basis: float32 [64, 32, 24, 512], P('sub', 'region'), may hold values from -0.25 to 0.25
- match_south: int32 [64, 32, 128], P('sub', 'region'), may hold values from 0 to 127, each once within a row
- match_east: int32 [64, 32, 128], P('sub', 'region'), may hold values from 0 to 127, each once within a row
- primal_index: int32 [64, 32, 24], P('sub', 'region'), may hold values from 0 to 383
- stiffness: int32 [64, 32], replicated, may hold values from 1 to 16
- level2_inverse: float32 [32, 384, 384], P('region', 'sub'), may hold values from -0.3125 to 0.3125
- level2_basis: float32 [32, 60, 384], P('region'), may hold values from -0.3125 to 0.3125
- top_inverse: float32 [1920, 1920], P(None, 'region'), as said below
Outputs:
- preconditioned: float32 [64, 32, 32, 512], P('sub', 'region')
The draws below stay inside these ranges and needn't reach their ends.
Inputs may be any that keep to these rules, and one draw needn't show every extreme that they name: top_inverse is symmetric.
All inputs are finite; a program needn't handle non-finite values.
Results may differ from the reference program's by a relative error of at most 0.000053.
Values sent between devices are 32-bit elements; how exact they have to be, the bound alone decides.
A program may use at most 64 MiB of HBM per device.

```python
import math
import jax
import jax.numpy as jnp
from jax import lax

B = 512
H = 128
K = 32
C1 = 24
P2 = 60
NA = 64
NB = 32
NP2 = 384
NT = 1920


def draw_top_inverse(key, part):
    key = jax.random.fold_in(key, 7)
    base = jax.random.normal(key, (NT, NT), jnp.float32)
    rows = lax_rows = jnp.arange(NT, dtype=jnp.int32)
    diagonal = (rows[:, None] == lax_rows[None, :]).astype(jnp.float32)
    return (base + base.T) * (1.0 / math.sqrt(2.0 * NT)) + diagonal


def with_ends(result, own_key, smallest, high):
    index_at = [jax.random.randint(jax.random.fold_in(own_key, axis), (), 0, length) for axis, length in enumerate(result.shape)]
    widest = result.shape.index(max(result.shape))
    next_to = index_at[:widest] + [(index_at[widest] + 1) % result.shape[widest]] + index_at[widest + 1:]
    return result.at[tuple(index_at)].set(smallest).at[tuple(next_to)].set(high)


def shard_levels(key, extent, shards, low, top_value):
    def one(axis_at, blocks):
        steps = jax.random.uniform(jax.random.fold_in(jax.random.fold_in(key, 6), axis_at), (blocks,), jnp.float32, low / len(shards), top_value / len(shards))
        return jnp.repeat(jnp.exp(steps), extent[axis_at] // blocks).reshape((-1,) + (1,) * (len(extent) - axis_at - 1))

    loudness = one(*shards[0])
    for cut in shards[1:]:
        loudness = loudness * one(*cut)
    return loudness


def noise(stream_key, extent, scale, bound, split=(), kind=jnp.bfloat16):
    result = jax.random.normal(stream_key, extent, jnp.float32) * scale
    if len(split) > 0:
        result = shard_levels(stream_key, extent, split, -0.22, 0.18) * result
    return jnp.clip(result, min=-bound, max=bound).astype(kind)


def setup_inputs(seed: int = 0) -> dict:
    splits = jax.random.split(jax.random.key(seed), 11)
    pieces = noise(splits[0], (NA, NB, K, B), 1.0, 6.0, ((0, 8), (1, 32)), jnp.float32)
    local_inverse = noise(splits[1], (NA, NB, B, B), B ** -0.5, 0.25, ((0, 8), (1, 32)), jnp.float32)
    primal_basis = noise(splits[2], (NA, NB, C1, B), B ** -0.5, 0.25, ((0, 8), (1, 32)), jnp.float32)
    match_south = jax.vmap(lambda own: jax.random.permutation(own, H))(jax.random.split(splits[3], NA * NB)).reshape((NA, NB, H)).astype(jnp.int32)
    match_east = jax.vmap(lambda own: jax.random.permutation(own, H))(jax.random.split(splits[4], NA * NB)).reshape((NA, NB, H)).astype(jnp.int32)
    primal_index = with_ends(jax.random.randint(splits[5], (NA, NB, C1), 0, NP2), jax.random.fold_in(splits[5], 1), 0, NP2 - 1).astype(jnp.int32)
    stiffness = with_ends(jax.random.randint(splits[6], (NA, NB), 1, 17), jax.random.fold_in(splits[6], 1), 1, 16).astype(jnp.int32)
    level2_inverse = noise(splits[7], (NB, NP2, NP2), NP2 ** -0.5, 0.3125, ((0, 32), (1, 8)), jnp.float32)
    level2_basis = noise(splits[8], (NB, P2, NP2), NP2 ** -0.5, 0.3125, ((0, 32),), jnp.float32)
    top_inverse = draw_top_inverse(jax.random.fold_in(splits[10], 71), 0)
    return {"pieces": pieces, "local_inverse": local_inverse, "primal_basis": primal_basis, "match_south": match_south, "match_east": match_east, "primal_index": primal_index, "stiffness": stiffness, "level2_inverse": level2_inverse, "level2_basis": level2_basis, "top_inverse": top_inverse}


HIGH = lax.Precision.HIGHEST


def pick_rows(values, order):
    return jnp.take_along_axis(values, jnp.broadcast_to(order[:, :, None, :].astype(jnp.int32), values.shape), axis=3)


def assemble(values, match_south, match_east):
    width = B // 4
    north_face = values[..., :width]
    south_face = values[..., width:2 * width]
    west_face = values[..., 2 * width:3 * width]
    east_face = values[..., 3 * width:]
    inv_south = jnp.argsort(match_south, axis=-1).astype(jnp.int32)
    inv_east = jnp.argsort(match_east, axis=-1).astype(jnp.int32)
    sent_south = pick_rows(south_face, inv_south)
    sent_east = pick_rows(east_face, inv_east)
    zero_row = jnp.zeros_like(north_face[:1])
    from_north = jnp.concatenate([zero_row, sent_south[:-1]], axis=0)
    next_north = jnp.concatenate([north_face[1:], zero_row], axis=0)
    from_south = pick_rows(next_north, match_south)
    zero_col = jnp.zeros_like(west_face[:, :1])
    from_west = jnp.concatenate([zero_col, sent_east[:, :-1]], axis=1)
    next_west = jnp.concatenate([west_face[:, 1:], zero_col], axis=1)
    from_east = pick_rows(next_west, match_east)
    return values + jnp.concatenate([from_north, from_south, from_west, from_east], axis=-1)


def face_weights(stiffness):
    stiff_vals = stiffness.astype(jnp.float32)
    padded = jnp.pad(stiff_vals, 1)
    ratios = jnp.stack([
        stiff_vals / (stiff_vals + padded[:-2, 1:-1]),
        stiff_vals / (stiff_vals + padded[2:, 1:-1]),
        stiff_vals / (stiff_vals + padded[1:-1, :-2]),
        stiff_vals / (stiff_vals + padded[1:-1, 2:])], axis=-1)
    return jnp.repeat(ratios, B // 4, axis=-1)


def reference(pieces, local_inverse, primal_basis, match_south, match_east, primal_index, stiffness, level2_inverse, level2_basis, top_inverse):
    row_weight = face_weights(stiffness)[:, :, None, :]
    scaled = assemble(pieces, match_south, match_east) * row_weight
    local_fix = jnp.einsum('abkx,abxy->abky', scaled, local_inverse, precision=HIGH)
    coarse_in = jnp.einsum('abkx,abix->abki', scaled, primal_basis, precision=HIGH)
    lookup = (primal_index[..., None] == jnp.arange(NP2, dtype=jnp.int32)).astype(jnp.float32)
    level_two_in = jnp.einsum('abki,abin->bkn', coarse_in, lookup, precision=HIGH)
    top_in = jnp.einsum('bkn,btn->bkt', level_two_in, level2_basis, precision=HIGH)
    top_flat = jnp.transpose(top_in, (1, 0, 2)).reshape(K, NT)
    top_fix = jnp.dot(top_flat, top_inverse, precision=HIGH)
    top_blocks = jnp.transpose(top_fix.reshape(K, NB, P2), (1, 0, 2))
    lifted = jnp.einsum('bkn,bnm->bkm', level_two_in, level2_inverse, precision=HIGH)
    lifted = lifted + jnp.einsum('bkt,btn->bkn', top_blocks, level2_basis, precision=HIGH)
    spread = jnp.einsum('bkn,abin->abki', lifted, lookup, precision=HIGH)
    combined = local_fix + jnp.einsum('abki,abix->abkx', spread, primal_basis, precision=HIGH)
    return assemble(combined * row_weight, match_south, match_east)
```

```python
import functools

import jax
import jax.numpy as jnp
from jax import lax
from jax.experimental import pallas as pl
from jax.experimental.pallas import tpu as pltpu
from jax.sharding import PartitionSpec as P

H = 128
MESH = pl.DeviceIdType.MESH
F32 = jnp.float32
BF16 = jnp.bfloat16


def split(x):
    high = x.astype(BF16)
    return high, (x - high.astype(F32)).astype(BF16)


def nn(a, b):
    return jnp.dot(a, b, preferred_element_type=F32)


def nt(a, b):
    return lax.dot_general(a, b, (((1,), (1,)), ((), ())), preferred_element_type=F32)


def three(product, x, high, low):
    rows = x.shape[0]
    x_high, x_low = split(x)
    both = product(jnp.concatenate([x_high, x_low], axis=0), high)
    return both[:rows] + both[rows:] + product(x_high, low)


def pick(face, order):
    return jnp.take_along_axis(face, jnp.broadcast_to(order, face.shape), axis=1)


def kernel(
    S, R, NL, K, C1, P2, N2,
    pieces, local_inverse, basis, match_south, match_east, primal_index, stiffness,
    level2_inverse, level2_basis, top_inverse,
    out,
    pc, inv, bas, south, east, index, stiff, l2inv, l2b, l2pad, topv,
    colpad, weight, unsouth, uneast,
    look, lbb_high, lbb_low, lb_stack, t_high, t_low, inv_high, inv_low,
    sent_south, sent_east, got_west, got_east, got_north, got_south,
    asm, fixed, part, part_got, rows_sent, rows_got, lift_own, lift_got,
    top_sent, top_got, cast_own, cast_got, lhs, fix_own, fix_got, two, tf,
    comb, sent_south2, sent_east2, got_west2, got_east2, got_north2, got_south2,
    load_sem, edge_send, edge_recv, small_send, small_recv, step_send, step_recv,
):
    s = lax.axis_index("sub")
    b = lax.axis_index("region")
    G = K // S
    OWN = N2 // S
    north_of, south_of = (lax.rem(s + S - 1, S), b), (lax.rem(s + 1, S), b)
    west_of, east_of = (s, lax.rem(b + R - 1, R)), (s, lax.rem(b + 1, R))

    barrier = pltpu.get_barrier_semaphore()

    def tell_region(i, c):
        pl.semaphore_signal(barrier, inc=1, device_id=(s, lax.rem(b + i, R)), device_id_type=MESH)
        return c

    def tell_sub(i, c):
        pl.semaphore_signal(barrier, inc=1, device_id=(lax.rem(s + i, S), b), device_id_type=MESH)
        return c

    lax.fori_loop(1, R, tell_region, 0)
    lax.fori_loop(1, S, tell_sub, 0)

    l2inv[...] = jnp.zeros_like(l2inv)
    topv[R * P2:, :] = jnp.zeros_like(topv[R * P2:, :])
    loads = [
        pltpu.make_async_copy(match_east.at[:, 0], east, load_sem.at[0]),
        pltpu.make_async_copy(match_south.at[:, 0], south, load_sem.at[1]),
        pltpu.make_async_copy(pieces.at[:, 0], pc, load_sem.at[2]),
        pltpu.make_async_copy(stiffness, stiff, load_sem.at[3]),
        pltpu.make_async_copy(primal_index.at[:, 0], index, load_sem.at[4]),
        pltpu.make_async_copy(basis.at[:, 0], bas, load_sem.at[5]),
        pltpu.make_async_copy(level2_basis.at[0], l2b, load_sem.at[6]),
        pltpu.make_async_copy(level2_inverse.at[0], l2inv.at[pl.ds(0, OWN)], load_sem.at[7]),
        pltpu.make_async_copy(top_inverse, topv.at[pl.ds(0, R * P2)], load_sem.at[8]),
        pltpu.make_async_copy(local_inverse.at[:, 0], inv, load_sem.at[9]),
    ]
    for load in loads:
        load.start()

    lane = lax.broadcasted_iota(jnp.int32, (K, H), 1).astype(F32).astype(BF16)
    face_row = lax.broadcasted_iota(jnp.int32, (H, H), 0)

    def invert(order):
        hit = (face_row == order).astype(F32).astype(BF16)
        return nt(lane, hit).astype(jnp.int32)

    loads[0].wait()
    for a in range(NL):
        uneast[a] = invert(east[a:a + 1, :])
    loads[1].wait()
    for a in range(NL):
        unsouth[a] = invert(south[a:a + 1, :])
    loads[2].wait()
    for a in range(NL):
        sent_east[a] = pick(pc[a, :, 3 * H:], uneast[a])
    sent_south[...] = pick(pc[NL - 1, :, H:2 * H], unsouth[NL - 1])

    pl.semaphore_wait(barrier, R - 1 + S - 1)

    def remote(src, dst, send, recv, device):
        return pltpu.make_async_remote_copy(
            src_ref=src, dst_ref=dst, send_sem=send, recv_sem=recv, device_id=device,
            device_id_type=MESH)

    def edges(phase, values, east_buf, south_buf, west_got, east_got, north_got, south_got):
        def to_west(a):
            return remote(values.at[a, :, pl.ds(2 * H, H)], east_got.at[a],
                          edge_send.at[phase, 0, a], edge_recv.at[phase, 0, a], west_of)

        def to_east(a):
            return remote(east_buf.at[a], west_got.at[a],
                          edge_send.at[phase, 1, a], edge_recv.at[phase, 1, a], east_of)

        to_north = remote(values.at[0, :, pl.ds(0, H)], south_got,
                          small_send.at[phase, 0], small_recv.at[phase, 0], north_of)
        to_south = remote(south_buf, north_got,
                          small_send.at[phase, 1], small_recv.at[phase, 1], south_of)
        return to_west, to_east, to_north, to_south

    to_west, to_east, to_north, to_south = edges(
        0, pc, sent_east, sent_south, got_west, got_east, got_north, got_south)
    for a in range(NL):
        to_west(a).start()
        to_east(a).start()
    to_north.start()
    to_south.start()

    loads[3].wait()
    levels = stiff[...].astype(F32)
    place = lax.broadcasted_iota(jnp.int32, levels.shape, 1)

    def column(position):
        return jnp.sum(jnp.where(place == position, levels, 0.0), axis=1, keepdims=True)

    total = levels.shape[0]
    colpad[...] = jnp.zeros_like(colpad)
    for at, position in enumerate((b, b - 1, b + 1)):
        colpad[at, 8:8 + total, :] = jnp.broadcast_to(column(position), (total, H))
    near = colpad[0, pl.ds(pl.multiple_of(s * NL, NL), NL + 16), :]
    own = near[8:8 + NL]
    start = pl.multiple_of(s * NL + 8, 8)
    weight[:, 0:H] = own / (own + near[7:7 + NL])
    weight[:, H:2 * H] = own / (own + near[9:9 + NL])
    weight[:, 2 * H:3 * H] = own / (own + colpad[1, pl.ds(start, NL), :])
    weight[:, 3 * H:] = own / (own + colpad[2, pl.ds(start, NL), :])

    loads[4].wait()
    loads[5].wait()
    loads[6].wait()
    l2pad[...] = jnp.zeros_like(l2pad)
    l2pad[0:P2, :] = l2b[...]
    l2_high, l2_low = split(l2pad[...])
    lb_stack[0:64, :] = l2_high
    lb_stack[64:128, :] = l2_low
    unknown = lax.broadcasted_iota(jnp.int32, (N2, C1), 0)
    odd = lax.rem(b, 2)
    lbb_high[...] = jnp.zeros_like(lbb_high)
    lbb_low[...] = jnp.zeros_like(lbb_low)
    half = pl.ds(pl.multiple_of(odd * 64, 64), 64)
    for a in range(NL):
        hit = (unknown == index[a:a + 1, :]).astype(F32).astype(BF16)
        look[a] = hit
        lb = nn(lb_stack[...], hit)
        lb_high, lb_low = lb[:64].astype(BF16), lb[64:].astype(BF16)
        b_high, b_low = split(bas[a])
        both = nn(jnp.concatenate([lb_high, lb_low], axis=0), b_high)
        lbb = (both[:64] + both[64:] + nn(lb_high, b_low)) * weight[a:a + 1, :]
        high, low = split(lbb)
        lbb_high[half, 4 * H * a:4 * H * (a + 1)] = high
        lbb_low[half, 4 * H * a:4 * H * (a + 1)] = low

    loads[8].wait()

    def spread_top(p, c):
        block = topv[pl.ds(pl.multiple_of(2 * P2 * p, 8), 2 * P2 + 8), :]
        pair = jnp.concatenate([block[0:64], block[P2:P2 + 64]], axis=0)
        high, low = split(pair)
        at = pl.ds(pl.multiple_of(128 * p, 128), 128)
        t_high[at, :] = high
        t_low[at, :] = low
        return c

    lax.fori_loop(0, R // 2, spread_top, 0)

    def masked(condition, value):
        return jnp.where(condition, value, jnp.zeros_like(value))

    to_north.wait_recv()
    to_south.wait_recv()
    for a in range(NL):
        before = masked(s > 0, got_north[...]) if a == 0 else pick(
            pc[a - 1, :, H:2 * H], unsouth[a - 1])
        after = pick(masked(s < S - 1, got_south[...]) if a == NL - 1 else pc[a + 1, :, 0:H],
                     south[a:a + 1, :])
        at = 4 * H * a
        asm[:, at:at + H] = pc[a, :, 0:H] + before
        asm[:, at + H:at + 2 * H] = pc[a, :, H:2 * H] + after
    for a in range(NL):
        at = 4 * H * a
        to_east(a).wait_recv()
        asm[:, at + 2 * H:at + 3 * H] = pc[a, :, 2 * H:3 * H] + masked(b > 0, got_west[a])
        to_west(a).wait_recv()
        asm[:, at + 3 * H:at + 4 * H] = pc[a, :, 3 * H:] + masked(
            b < R - 1, pick(got_east[a], east[a:a + 1, :]))

    top = three(nt, asm[...], lbb_high[...], lbb_low[...])
    for g in range(S):
        top_sent[g] = top[G * g:G * (g + 1)]

    def others(count, me, make):
        def body(i, c):
            make(lax.rem(me + i, count)).start()
            return c
        lax.fori_loop(1, count, body, 0)

    def arrived(ref, count, sem):
        pltpu.make_async_copy(ref.at[pl.ds(0, count)], ref.at[pl.ds(0, count)], sem).wait()

    top_got[s] = top_sent[s]
    others(S, s, lambda o: remote(
        top_sent.at[o], top_got.at[s], step_send.at[0], step_recv.at[0], (o, b)))

    two_in = jnp.zeros((K, N2), F32)
    for a in range(NL):
        scaled = asm[:, 4 * H * a:4 * H * (a + 1)] * weight[a:a + 1, :]
        asm[:, 4 * H * a:4 * H * (a + 1)] = scaled
        b_high, b_low = split(bas[a])
        c_high, c_low = split(three(nt, scaled, b_high, b_low))
        both = nt(jnp.concatenate([c_high, c_low], axis=0), look[a])
        two_in += both[:K] + both[K:]
    for g in range(S):
        turned = two_in if g == 0 else pltpu.roll(two_in, N2 - OWN * g, 1)
        part[g] = turned[:, 0:H]
    part_got[s] = part[s]
    others(S, s, lambda o: remote(
        part.at[o], part_got.at[s], step_send.at[1], step_recv.at[1], (o, b)))

    arrived(top_got, S - 1, step_recv.at[0])
    mine = top_got[0]
    for g in range(1, S):
        mine += top_got[g]
    cast_own[...] = mine
    cast_got[b] = mine

    def cast(i, c):
        o = lax.rem(b + R // 2 + i, R)

        remote(cast_own, cast_got.at[b], step_send.at[2], step_recv.at[2], (s, o)).start()
        return c

    lax.fori_loop(0, R // 2, cast, 0)
    lax.fori_loop(R // 2 + 1, R, cast, 0)

    loads[9].wait()

    def solve(a, c):
        high, low = split(inv[a])
        at = pl.ds(pl.multiple_of(4 * H * a, 4 * H), 4 * H)
        fixed[:, at] = three(nn, asm[:, at], high, low)
        return c

    lax.fori_loop(0, NL // 2, solve, 0)

    loads[7].wait()
    arrived(part_got, S - 1, step_recv.at[1])
    own_two = part_got[0]
    for g in range(1, S):
        own_two += part_got[g]
    i_high, i_low = split(l2inv[...])
    lift = three(nn, own_two, i_high, i_low)
    for g in range(S):
        rows_sent[g] = lift[G * g:G * (g + 1)]
    rows_got[s] = rows_sent[s]
    others(S, s, lambda o: remote(
        rows_sent.at[o], rows_got.at[s], step_send.at[3], step_recv.at[3], (o, b)))
    lax.fori_loop(NL // 2, NL, solve, 0)
    arrived(rows_got, S - 1, step_recv.at[3])
    lift4 = rows_got[0]
    for g in range(1, S):
        lift4 += rows_got[g]
    lift_own[...] = lift4
    lift_got[s] = lift4
    others(S, s, lambda o: remote(
        lift_own, lift_got.at[s], step_send.at[4], step_recv.at[4], (o, b)))

    arrived(cast_got, R - 1, step_recv.at[2])
    for p in range(R // 2):
        pair = cast_got[2 * p] + cast_got[2 * p + 1]
        high = pair.astype(BF16).astype(F32)
        lhs[0:G, H * p:H * (p + 1)] = high
        lhs[G:2 * G, H * p:H * (p + 1)] = pair - high
    left = lhs[...].astype(BF16)
    first = nn(left, t_high[...])
    fix = first[0:G] + first[G:2 * G] + nn(left, t_low[...])[0:G]
    fix_own[...] = jnp.zeros_like(fix_own)
    fix_own[:, 0:P2] = fix
    fix = fix_own[...]
    fix = jnp.where(odd == 1, pltpu.roll(fix, 64, 1), fix)
    fix_own[...] = fix
    fix_got[s] = fix
    others(S, s, lambda o: remote(
        fix_own, fix_got.at[s], step_send.at[5], step_recv.at[5], (o, b)))

    arrived(lift_got, S - 1, step_recv.at[4])
    for g in range(S):
        two[G * g:G * (g + 1), :] = lift_got[g]
    two_high, two_low = split(two[...])
    two_both = jnp.concatenate([two_high, two_low], axis=0)
    for a in range(NL):
        e = nn(two_both, look[a])
        b_high, b_low = split(bas[a])
        at = 4 * H * a
        fixed[:, at:at + 4 * H] = (fixed[:, at:at + 4 * H] + three(
            nn, e[:K] + e[K:], b_high, b_low)) * weight[a:a + 1, :]

    arrived(fix_got, S - 1, step_recv.at[5])
    for g in range(S):
        tf[G * g:G * (g + 1), :] = fix_got[g]
    f_high, f_low = split(tf[...])
    f_both = jnp.concatenate([f_high, f_low], axis=0)

    to_west2, to_east2, to_north2, to_south2 = edges(
        1, comb, sent_east2, sent_south2, got_west2, got_east2, got_north2, got_south2)
    for a in range(NL):
        at = 4 * H * a
        both = nn(f_both, lbb_high[:, at:at + 4 * H])
        value = fixed[:, at:at + 4 * H] + both[:K] + both[K:] + nn(
            f_high, lbb_low[:, at:at + 4 * H])
        comb[a] = value
        to_west2(a).start()
        sent_east2[a] = pick(value[:, 3 * H:], uneast[a])
        to_east2(a).start()
        if a == 0:
            to_north2.start()
        if a == NL - 1:
            sent_south2[...] = pick(value[:, H:2 * H], unsouth[a])
            to_south2.start()

    to_north2.wait_recv()
    to_south2.wait_recv()
    for a in range(NL):
        before = masked(s > 0, got_north2[...]) if a == 0 else pick(
            comb[a - 1, :, H:2 * H], unsouth[a - 1])
        after = pick(masked(s < S - 1, got_south2[...]) if a == NL - 1 else comb[a + 1, :, 0:H],
                     south[a:a + 1, :])
        out[a, 0, :, 0:H] = comb[a, :, 0:H] + before
        out[a, 0, :, H:2 * H] = comb[a, :, H:2 * H] + after
    for a in range(NL):
        to_east2(a).wait_recv()
        out[a, 0, :, 2 * H:3 * H] = comb[a, :, 2 * H:3 * H] + masked(b > 0, got_west2[a])
        to_west2(a).wait_recv()
        out[a, 0, :, 3 * H:] = comb[a, :, 3 * H:] + masked(
            b < R - 1, pick(got_east2[a], east[a:a + 1, :]))

    for first in ((to_west, to_east, to_north, to_south),
                  (to_west2, to_east2, to_north2, to_south2)):
        for a in range(NL):
            first[0](a).wait_send()
            first[1](a).wait_send()
        first[2].wait_send()
        first[3].wait_send()
    arrived(top_got, S - 1, step_send.at[0])
    arrived(part_got, S - 1, step_send.at[1])
    arrived(cast_got, R - 1, step_send.at[2])
    arrived(rows_got, S - 1, step_send.at[3])
    arrived(lift_got, S - 1, step_send.at[4])
    arrived(fix_got, S - 1, step_send.at[5])


def solution(mesh):
    S, R = mesh.shape["sub"], mesh.shape["region"]

    def on_device(*args):
        NL, _, K, B = args[0].shape
        C1 = args[2].shape[2]
        P2, N2 = args[8].shape[1:]
        NA = args[6].shape[0]
        G = K // S
        vm = pltpu.VMEM
        edge = [
            vm((K, H), F32), vm((NL, K, H), F32), vm((NL, K, H), F32), vm((NL, K, H), F32),
            vm((K, H), F32), vm((K, H), F32)]
        scratch = [
            vm((NL, K, B), F32), vm((NL, B, B), F32), vm((NL, C1, B), F32),
            vm((NL, H), jnp.int32), vm((NL, H), jnp.int32), vm((NL, C1), jnp.int32),
            vm(args[6].shape, jnp.int32), vm((H, N2), F32), vm((P2, N2), F32), vm((64, N2), F32),
            vm((R * P2 + 8, P2), F32),
            vm((3, NA + 16, H), F32), vm((NL, B), F32),
            vm((NL, K, H), jnp.int32), vm((NL, K, H), jnp.int32),
            vm((NL, N2, C1), BF16), vm((128, NL * B), BF16), vm((128, NL * B), BF16),
            vm((128, N2), BF16), vm((64 * R, P2), BF16), vm((64 * R, P2), BF16),
            vm((16, 128), BF16), vm((16, 128), BF16),
            *edge,
            vm((K, NL * B), F32), vm((K, NL * B), F32),
            vm((S, K, H), F32), vm((S, K, H), F32),
            vm((S, G, N2), F32), vm((S, G, N2), F32), vm((G, N2), F32), vm((S, G, N2), F32),
            vm((S, G, H), F32), vm((S, G, H), F32), vm((G, H), F32), vm((R, G, H), F32),
            vm((2 * G, R // 2 * H), F32), vm((G, H), F32), vm((S, G, H), F32),
            vm((K, N2), F32), vm((K, H), F32),
            vm((NL, K, B), F32), *edge,
            pltpu.SemaphoreType.DMA((10,)),
            pltpu.SemaphoreType.DMA((2, 2, NL)), pltpu.SemaphoreType.DMA((2, 2, NL)),
            pltpu.SemaphoreType.DMA((2, 2)), pltpu.SemaphoreType.DMA((2, 2)),
            pltpu.SemaphoreType.DMA((6,)), pltpu.SemaphoreType.DMA((6,)),
        ]
        return pl.pallas_call(
            functools.partial(kernel, S, R, NL, K, C1, P2, N2),
            out_shape=jax.ShapeDtypeStruct(args[0].shape, F32),
            in_specs=[pl.BlockSpec(memory_space=pl.ANY)] * len(args),
            out_specs=pl.BlockSpec(memory_space=pltpu.VMEM),
            scratch_shapes=scratch,
            compiler_params=pltpu.CompilerParams(
                collective_id=0, has_side_effects=True, vmem_limit_bytes=56 * 2**20),
        )(*args)

    in_specs = (
        P("sub", "region", None, None),
        P("sub", "region", None, None),
        P("sub", "region", None, None),
        P("sub", "region", None),
        P("sub", "region", None),
        P("sub", "region", None),
        P(),
        P("region", "sub", None),
        P("region", None, None),
        P(None, "region"),
    )
    out_specs = P("sub", "region", None, None)
    return jax.shard_map(
        on_device, mesh=mesh, in_specs=in_specs, out_specs=out_specs, check_vma=False
    )
```

```python
import functools

import jax
import jax.numpy as jnp
from jax import lax
from jax.experimental import pallas as pl
from jax.experimental.pallas import tpu as pltpu
from jax.sharding import PartitionSpec as P

H = 128
EARLY = 4
MESH = pl.DeviceIdType.MESH
F32 = jnp.float32
BF16 = jnp.bfloat16


def split(x):
    high = x.astype(BF16)
    return high, (x - high.astype(F32)).astype(BF16)


def nn(a, b):
    return jnp.dot(a, b, preferred_element_type=F32)


def nt(a, b):
    return lax.dot_general(a, b, (((1,), (1,)), ((), ())), preferred_element_type=F32)


def three(product, x, high, low):
    rows = x.shape[0]
    x_high, x_low = split(x)
    both = product(jnp.concatenate([x_high, x_low], axis=0), high)
    return both[:rows] + both[rows:] + product(x_high, low)


def pick(face, order):
    return jnp.take_along_axis(face, jnp.broadcast_to(order, face.shape), axis=1)


def kernel(
    S, R, NL, K, C1, P2, N2,
    pieces, local_inverse, basis, match_south, match_east, primal_index, stiffness,
    level2_inverse, level2_basis, top_inverse,
    out,
    pc, inv, bas, south, east, north_table, west_table, index, stiff, l2inv, l2b, l2pad, topt, topv,
    weight, unsouth, unwest,
    look, lbb_high, lbb_low, lb_stack, t_high, t_low,
    got_west, got_east, got_north, got_south,
    asm, fixed, lhs_two, rows_sent, rows_got, lift_own, lift_got,
    top_sent, top_got, cast_own, cast_got, lhs, fix_own, fix_got, two, tf,
    comb, got_west2, got_east2, got_north2, got_south2,
    weight_near, bas_west, bas_east, bas_north, bas_south, index_west, index_east, index_north,
    index_south, l2_west, l2_east, slots, looks, big_b_high, big_b_low, big_q_high, big_q_low,
    fix_rolled, more_send, more_recv,
    load_sem, edge_send, edge_recv, small_send, small_recv, step_send, step_recv,
):
    s = lax.axis_index("sub")
    b = lax.axis_index("region")
    G = K // S
    OWN = N2 // S
    north_of, south_of = (lax.rem(s + S - 1, S), b), (lax.rem(s + 1, S), b)
    west_of, east_of = (s, lax.rem(b + R - 1, R)), (s, lax.rem(b + 1, R))

    barrier = pltpu.get_barrier_semaphore()

    def tell_region(i, c):
        pl.semaphore_signal(barrier, inc=1, device_id=(s, lax.rem(b + i, R)), device_id_type=MESH)
        return c

    def tell_sub(i, c):
        for region in (b, east_of[1], west_of[1]):
            pl.semaphore_signal(
                barrier, inc=1, device_id=(lax.rem(s + i, S), region), device_id_type=MESH)
        return c

    own_rows = pl.ds(pl.multiple_of(s * OWN, 8), OWN)
    loads = [
        pltpu.make_async_copy(match_east.at[:, 0], east, load_sem.at[0]),
        pltpu.make_async_copy(match_south.at[:, 0], south, load_sem.at[1]),
        pltpu.make_async_copy(pieces.at[:, 0], pc, load_sem.at[2]),
        pltpu.make_async_copy(stiffness, stiff, load_sem.at[3]),
        pltpu.make_async_copy(primal_index.at[:, 0], index, load_sem.at[4]),
        pltpu.make_async_copy(basis.at[:, 0], bas, load_sem.at[5]),
        pltpu.make_async_copy(level2_basis.at[:, 0], l2b, load_sem.at[6]),
        pltpu.make_async_copy(level2_inverse.at[0], l2inv.at[own_rows], load_sem.at[7]),
        pltpu.make_async_copy(top_inverse, topt, load_sem.at[8]),
        pltpu.make_async_copy(local_inverse.at[:, 0], inv, load_sem.at[9]),
    ]
    lax.fori_loop(1, R, tell_region, 0)
    lax.fori_loop(1, S, tell_sub, 0)
    for load in loads:
        load.start()
    pl.semaphore_wait(barrier, R - 1 + 3 * (S - 1))

    def remote(src, dst, send, recv, device):
        return pltpu.make_async_remote_copy(
            src_ref=src, dst_ref=dst, send_sem=send, recv_sem=recv, device_id=device,
            device_id_type=MESH)

    def edges(phase, face, west_got, east_got, north_got, south_got):
        def to_west(a):
            return remote(face(a, 2), east_got.at[a],
                          edge_send.at[phase, 0, a], edge_recv.at[phase, 0, a], west_of)

        def to_east(a):
            return remote(face(a, 3), west_got.at[a],
                          edge_send.at[phase, 1, a], edge_recv.at[phase, 1, a], east_of)

        to_north = remote(face(0, 0), south_got,
                          small_send.at[phase, 0], small_recv.at[phase, 0], north_of)
        to_south = remote(face(NL - 1, 1), north_got,
                          small_send.at[phase, 1], small_recv.at[phase, 1], south_of)
        return to_west, to_east, to_north, to_south

    to_west, to_east, to_north, to_south = edges(
        0, lambda a, f: pieces.at[a, 0, :, pl.ds(f * H, H)],
        got_west, got_east, got_north, got_south)
    table_east = remote(match_east.at[:, 0], west_table,
                        small_send.at[0, 2], small_recv.at[0, 2], east_of)
    table_south = remote(match_south.at[NL - 1], north_table,
                         small_send.at[0, 3], small_recv.at[0, 3], south_of)
    table_east.start()
    table_south.start()
    for a in range(NL):
        to_west(a).start()
        to_east(a).start()
    to_north.start()
    to_south.start()

    def others(count, me, make):
        def body(i, c):
            make(lax.rem(me + i, count)).start()
            return c
        lax.fori_loop(1, count, body, 0)

    others(S, s, lambda o: remote(
        level2_inverse.at[0], l2inv.at[own_rows], step_send.at[3], step_recv.at[3], (o, b)))

    def face(f):
        return basis.at[:, 0, :, pl.ds(f * H, H)]

    more = [(face(3), bas_west, east_of), (primal_index.at[:, 0], index_west, east_of),
            (level2_basis.at[:, 0], l2_west, east_of),
            (face(2), bas_east, west_of), (primal_index.at[:, 0], index_east, west_of),
            (level2_basis.at[:, 0], l2_east, west_of),
            (basis.at[NL - 1, 0, :, pl.ds(H, H)], bas_north, south_of),
            (primal_index.at[NL - 1], index_north, south_of),
            (basis.at[0, 0, :, pl.ds(0, H)], bas_south, north_of),
            (primal_index.at[0], index_south, north_of)]
    more = [remote(src, dst, more_send.at[i], more_recv.at[i], device)
            for i, (src, dst, device) in enumerate(more)]
    for copy in more:
        copy.start()

    lane = lax.broadcasted_iota(jnp.int32, (K, H), 1).astype(F32).astype(BF16)
    face_row = lax.broadcasted_iota(jnp.int32, (H, H), 0)

    def invert(order):
        hit = (face_row == order).astype(F32).astype(BF16)
        return nt(lane, hit).astype(jnp.int32)

    loads[0].wait()
    loads[1].wait()
    for a in range(NL - 1):
        unsouth[a] = invert(south[a:a + 1, :])

    loads[3].wait()
    levels = stiff[...].astype(F32)
    regions = lax.broadcasted_iota(jnp.int32, levels.shape, 0)
    spots = (lax.broadcasted_iota(jnp.int32, (NL, levels.shape[1]), 1)
             - lax.broadcasted_iota(jnp.int32, (NL, levels.shape[1]), 0) - s * NL)

    def level(region, step):
        row = jnp.sum(jnp.where(regions == region, levels, 0.0), axis=0, keepdims=True)
        return jnp.sum(jnp.where(spots == step, row, 0.0), axis=1, keepdims=True)

    own = level(b, 0)
    for f, other in enumerate((level(b, -1), level(b, 1), level(b - 1, 0), level(b + 1, 0))):
        weight[:, f * H:(f + 1) * H] = jnp.broadcast_to(own / (own + other), (NL, H))
        weight_near[:, f * H:(f + 1) * H] = jnp.broadcast_to(other / (own + other), (NL, H))

    loads[4].wait()
    loads[5].wait()
    loads[6].wait()
    l2pad[...] = jnp.zeros_like(l2pad)
    l2pad[0:P2, :] = l2b[...]
    l2_high, l2_low = split(l2pad[...])
    lb_stack[0:64, :] = l2_high
    lb_stack[64:128, :] = l2_low
    unknown = lax.broadcasted_iota(jnp.int32, (N2, C1), 0)
    odd = lax.rem(b, 2)
    lbb_high[...] = jnp.zeros_like(lbb_high)
    lbb_low[...] = jnp.zeros_like(lbb_low)
    half = pl.ds(pl.multiple_of(odd * 64, 64), 64)
    for a in range(NL):
        hit = (unknown == index[a:a + 1, :]).astype(F32).astype(BF16)
        look[a] = hit
        lb = nn(lb_stack[...], hit)
        lb_high, lb_low = lb[:64].astype(BF16), lb[64:].astype(BF16)
        b_high, b_low = split(bas[a])
        both = nn(jnp.concatenate([lb_high, lb_low], axis=0), b_high)
        lbb = (both[:64] + both[64:] + nn(lb_high, b_low)) * weight[a:a + 1, :]
        high, low = split(lbb)
        lbb_high[half, 4 * H * a:4 * H * (a + 1)] = high
        lbb_low[half, 4 * H * a:4 * H * (a + 1)] = low

    loads[8].wait()
    for c in range(R * P2 // 128):
        topv[128 * c:128 * (c + 1), :] = topt[:, 128 * c:128 * (c + 1)].T
    topv[R * P2:, :] = jnp.zeros_like(topv[R * P2:, :])

    def spread_top(p, c):
        block = topv[pl.ds(pl.multiple_of(2 * P2 * p, 8), 2 * P2 + 8), :]
        pair = jnp.concatenate([block[0:64], block[P2:P2 + 64]], axis=0)
        high, low = split(pair)
        at = pl.ds(pl.multiple_of(128 * p, 128), 128)
        t_high[at, :] = high
        t_low[at, :] = low
        return c

    lax.fori_loop(0, R // 2, spread_top, 0)

    def masked(condition, value):
        return jnp.where(condition, value, jnp.zeros_like(value))

    table_south.wait_recv()
    unsouth[NL - 1] = invert(north_table[...])
    table_east.wait_recv()
    for a in range(NL):
        unwest[a] = invert(west_table[a:a + 1, :])
    loads[2].wait()
    to_north.wait_recv()
    to_south.wait_recv()
    for a in range(NL):
        before = pick(masked(s > 0, got_north[...]) if a == 0 else pc[a - 1, :, H:2 * H],
                      unsouth[(a + NL - 1) % NL])
        after = pick(masked(s < S - 1, got_south[...]) if a == NL - 1 else pc[a + 1, :, 0:H],
                     south[a:a + 1, :])
        at = 4 * H * a
        asm[:, at:at + H] = pc[a, :, 0:H] + before
        asm[:, at + H:at + 2 * H] = pc[a, :, H:2 * H] + after
    for a in range(NL):
        at = 4 * H * a
        to_east(a).wait_recv()
        asm[:, at + 2 * H:at + 3 * H] = pc[a, :, 2 * H:3 * H] + masked(
            b > 0, pick(got_west[a], unwest[a]))
        to_west(a).wait_recv()
        asm[:, at + 3 * H:at + 4 * H] = pc[a, :, 3 * H:] + masked(
            b < R - 1, pick(got_east[a], east[a:a + 1, :]))

    top = three(nt, asm[...], lbb_high[...], lbb_low[...])
    for g in range(S):
        top_sent[g] = top[G * g:G * (g + 1)]

    def arrived(ref, count, sem):
        pltpu.make_async_copy(ref.at[pl.ds(0, count)], ref.at[pl.ds(0, count)], sem).wait()

    top_got[s] = top_sent[s]
    others(S, s, lambda o: remote(
        top_sent.at[o], top_got.at[s], step_send.at[0], step_recv.at[0], (o, b)))

    two_in = jnp.zeros((K, N2), F32)
    for a in range(NL):
        scaled = asm[:, 4 * H * a:4 * H * (a + 1)] * weight[a:a + 1, :]
        asm[:, 4 * H * a:4 * H * (a + 1)] = scaled
        b_high, b_low = split(bas[a])
        c_high, c_low = split(three(nt, scaled, b_high, b_low))
        both = nt(jnp.concatenate([c_high, c_low], axis=0), look[a])
        two_in += both[:K] + both[K:]
    for g in range(S):
        rows_sent[g] = two_in[G * g:G * (g + 1)]
    rows_got[s] = rows_sent[s]
    others(S, s, lambda o: remote(
        rows_sent.at[o], rows_got.at[s], step_send.at[1], step_recv.at[1], (o, b)))

    to_west2, to_east2, to_north2, to_south2 = edges(
        1, lambda a, f: comb.at[a, :, pl.ds(f * H, H)],
        got_west2, got_east2, got_north2, got_south2)
    loads[9].wait()

    def solve(a, c):
        high, low = split(inv[a])
        at = pl.ds(pl.multiple_of(4 * H * a, 4 * H), 4 * H)
        comb[a] = three(nn, asm[:, at], high, low) * weight[pl.ds(a, 1), :]
        to_west2(a).start()
        to_east2(a).start()
        return c

    lax.fori_loop(0, EARLY, solve, 0)

    arrived(top_got, S - 1, step_recv.at[0])
    mine = top_got[0]
    for g in range(1, S):
        mine += top_got[g]
    cast_own[...] = mine
    cast_got[b] = mine

    def cast(i, c):
        o = lax.rem(b + R // 2 + i, R)

        remote(cast_own, cast_got.at[b], step_send.at[2], step_recv.at[2], (s, o)).start()
        return c

    lax.fori_loop(0, R // 2, cast, 0)
    lax.fori_loop(R // 2 + 1, R, cast, 0)

    lax.fori_loop(EARLY, NL, solve, 0)
    to_north2.start()
    to_south2.start()

    loads[7].wait()
    arrived(l2inv, (S - 1) * OWN, step_recv.at[3])
    i_high, i_low = split(l2inv[...])
    arrived(rows_got, S - 1, step_recv.at[1])
    two_mine = rows_got[0]
    for g in range(1, S):
        two_mine += rows_got[g]
    high = two_mine.astype(BF16).astype(F32)
    lhs_two[0:G, :] = high
    lhs_two[G:2 * G, :] = two_mine - high
    left = lhs_two[...].astype(BF16)
    first = nn(left, i_high)
    lift4 = first[0:G] + first[G:2 * G] + nn(left, i_low)[0:G]
    lift_own[...] = lift4
    lift_got[s] = lift4

    def spread(i, src, rolled, got, k):
        o = lax.rem(s + i, S)
        remote(rolled, got.at[S + s], step_send.at[k], step_recv.at[k], (o, east_of[1])).start()
        remote(src, got.at[2 * S + s], step_send.at[k], step_recv.at[k], (o, west_of[1])).start()

    def to_three_regions(src, rolled, got, k):
        def body(i, c):
            spread(i, src, rolled, got, k)
            o = lax.rem(s + i, S)
            remote(src, got.at[s], step_send.at[k], step_recv.at[k], (o, b)).start()
            return c
        lax.fori_loop(1, S, body, 0)
        spread(0, src, rolled, got, k)

    to_three_regions(lift_own, lift_own, lift_got, 4)

    for copy in more:
        copy.wait_recv()
    slots[...] = jnp.full_like(slots, -1)
    slots[:, 0:C1] = index[...]
    slots[0:1, C1:2 * C1] = index_north[...]
    slots[1:NL, C1:2 * C1] = index[0:NL - 1, :]
    slots[0:NL - 1, 2 * C1:3 * C1] = index[1:NL, :]
    slots[NL - 1:NL, 2 * C1:3 * C1] = index_south[...]
    slots[:, 3 * C1:4 * C1] = index_west[...]
    slots[:, 4 * C1:5 * C1] = index_east[...]
    stacks = [lb_stack[...]]
    for level2 in (l2_west, l2_east):
        l2pad[0:P2, :] = level2[...]
        stacks.append(jnp.concatenate(split(l2pad[...]), axis=0))
    spot = lax.broadcasted_iota(jnp.int32, (N2, H), 1)
    unknown = lax.broadcasted_iota(jnp.int32, (N2, H), 0)
    big_q_high[:, 192:256, :] = jnp.zeros_like(big_q_high[:, 192:256, :])
    big_q_low[:, 192:256, :] = jnp.zeros_like(big_q_low[:, 192:256, :])
    gap = jnp.zeros((C1, H), F32)
    for a in range(NL):
        hit = jnp.where(unknown == slots[a:a + 1, :], 1.0, 0.0)
        lb_high, lb_low = [], []
        for j, (low_end, high_end) in enumerate(((0, 3), (3, 4), (4, 5))):
            own_hit = jnp.where((spot >= low_end * C1) & (spot < high_end * C1), hit, 0.0).astype(BF16)
            looks[a, j * N2:(j + 1) * N2, :] = own_hit
            lb = nn(stacks[j], own_hit)
            lb_high.append(lb[0:64])
            lb_low.append(lb[64:128])
        north = bas_north[...] if a == 0 else bas[a - 1, :, H:2 * H]
        north_weight = weight_near[0:1, 0:H] if a == 0 else weight[a - 1:a, H:2 * H]
        after = bas_south[...] if a == NL - 1 else bas[a + 1, :, 0:H]
        after_weight = (weight_near[a:a + 1, H:2 * H] if a == NL - 1
                        else weight[a + 1:a + 2, 0:H])
        faces = [
            pick(north, unsouth[(a + NL - 1) % NL, 0:1, :]) * north_weight,
            pick(after, south[a:a + 1, :]) * after_weight,
            pick(bas_west[a], unwest[a, 0:1, :]) * weight_near[a:a + 1, 2 * H:3 * H],
            pick(bas_east[a], east[a:a + 1, :]) * weight_near[a:a + 1, 3 * H:]]
        rows = [bas[a] * weight[a:a + 1, :]]
        for f in range(4):
            rows.append(jnp.concatenate([gap] * f + [faces[f]] + [gap] * (3 - f), axis=1))
        rows.append(jnp.zeros((H - 5 * C1, 4 * H), F32))
        high, low = split(jnp.concatenate(rows, axis=0))
        big_b_high[a] = high
        big_b_low[a] = low
        q_high = jnp.concatenate(lb_high, axis=0).astype(BF16)
        q_low = jnp.concatenate(lb_low, axis=0).astype(BF16)
        both = nn(jnp.concatenate([q_high, q_low], axis=0), high)
        q_high, q_low = split(both[0:192] + both[192:] + nn(q_high, low))
        big_q_high[a, 0:192, :] = q_high
        big_q_low[a, 0:192, :] = q_low

    arrived(cast_got, R - 1, step_recv.at[2])
    for p in range(R // 2):
        pair = cast_got[2 * p] + cast_got[2 * p + 1]
        high = pair.astype(BF16).astype(F32)
        lhs[0:G, H * p:H * (p + 1)] = high
        lhs[G:2 * G, H * p:H * (p + 1)] = pair - high
    left = lhs[...].astype(BF16)
    first = nn(left, t_high[...])
    fix = first[0:G] + first[G:2 * G] + nn(left, t_low[...])[0:G]
    fix_own[...] = jnp.zeros_like(fix_own)
    fix_own[:, 0:P2] = fix
    fix = fix_own[...]
    fix_rolled[...] = pltpu.roll(fix, 64, 1)
    fix_got[s] = fix
    to_three_regions(fix_own, fix_rolled, fix_got, 5)

    to_north2.wait_recv()
    to_south2.wait_recv()
    for a in range(NL):
        before = pick(masked(s > 0, got_north2[...]) if a == 0 else comb[a - 1, :, H:2 * H],
                      unsouth[(a + NL - 1) % NL])
        after = pick(masked(s < S - 1, got_south2[...]) if a == NL - 1 else comb[a + 1, :, 0:H],
                     south[a:a + 1, :])
        to_east2(a).wait_recv()
        to_west2(a).wait_recv()
        west = masked(b > 0, pick(got_west2[a], unwest[a]))
        east_side = masked(b < R - 1, pick(got_east2[a], east[a:a + 1, :]))
        fixed[:, 4 * H * a:4 * H * (a + 1)] = comb[a] + jnp.concatenate(
            [before, after, west, east_side], axis=1)

    arrived(lift_got, 3 * S - 1, step_recv.at[4])
    for j in range(3):
        for g in range(S):
            two[G * g:G * (g + 1), j * N2:(j + 1) * N2] = lift_got[j * S + g]
    two_both = jnp.concatenate(split(two[...]), axis=0)
    for a in range(NL):
        e = nn(two_both, looks[a])
        at = 4 * H * a
        fixed[:, at:at + 4 * H] += three(nn, e[:K] + e[K:], big_b_high[a], big_b_low[a])

    arrived(fix_got, 3 * S - 1, step_recv.at[5])
    for g in range(S):
        tf[G * g:G * (g + 1), 0:H] = fix_got[g] + fix_got[S + g]
        tf[G * g:G * (g + 1), H:2 * H] = fix_got[2 * S + g]
    f_high, f_low = split(tf[...])
    f_both = jnp.concatenate([f_high, f_low], axis=0)
    for a in range(NL):
        both = nn(f_both, big_q_high[a])
        out[a, 0] = fixed[:, 4 * H * a:4 * H * (a + 1)] + both[:K] + both[K:] + nn(
            f_high, big_q_low[a])

    for first in ((to_west, to_east, to_north, to_south),
                  (to_west2, to_east2, to_north2, to_south2)):
        for a in range(NL):
            first[0](a).wait_send()
            first[1](a).wait_send()
        first[2].wait_send()
        first[3].wait_send()
    for copy in more:
        copy.wait_send()
    table_east.wait_send()
    table_south.wait_send()
    arrived(top_got, S - 1, step_send.at[0])
    arrived(rows_got, S - 1, step_send.at[1])
    arrived(cast_got, R - 1, step_send.at[2])
    arrived(l2inv, (S - 1) * OWN, step_send.at[3])
    arrived(lift_got, 3 * S - 1, step_send.at[4])
    arrived(fix_got, 3 * S - 1, step_send.at[5])


def solution(mesh):
    S, R = mesh.shape["sub"], mesh.shape["region"]

    def on_device(*args):
        NL, _, K, B = args[0].shape
        C1 = args[2].shape[2]
        P2, N2 = args[8].shape[1:]
        NA = args[6].shape[0]
        G = K // S
        vm = pltpu.VMEM
        edge = [vm((NL, K, H), F32), vm((NL, K, H), F32), vm((K, H), F32), vm((K, H), F32)]
        scratch = [
            vm((NL, K, B), F32), vm((NL, B, B), F32), vm((NL, C1, B), F32),
            vm((NL, H), jnp.int32), vm((NL, H), jnp.int32), vm((1, H), jnp.int32),
            vm((NL, H), jnp.int32), vm((NL, C1), jnp.int32), vm((R, NA), jnp.int32), vm((N2, N2), F32), vm((P2, N2), F32), vm((64, N2), F32),
            vm((P2, R * P2), F32), vm((R * P2 + 8, P2), F32), vm((NL, B), F32),
            vm((NL, K, H), jnp.int32), vm((NL, K, H), jnp.int32),
            vm((NL, N2, C1), BF16), vm((128, NL * B), BF16), vm((128, NL * B), BF16),
            vm((128, N2), BF16), vm((64 * R, P2), BF16), vm((64 * R, P2), BF16),
            *edge,
            vm((K, NL * B), F32), vm((K, NL * B), F32),
            vm((2 * G, N2), F32),
            vm((S, G, N2), F32), vm((S, G, N2), F32), vm((G, N2), F32), vm((3 * S, G, N2), F32),
            vm((S, G, H), F32), vm((S, G, H), F32), vm((G, H), F32), vm((R, G, H), F32),
            vm((2 * G, R // 2 * H), F32), vm((G, H), F32), vm((3 * S, G, H), F32),
            vm((K, 3 * N2), F32), vm((K, 2 * H), F32),
            vm((NL, K, B), F32), *edge,
            vm((NL, B), F32), vm((NL, C1, H), F32), vm((NL, C1, H), F32), vm((C1, H), F32),
            vm((C1, H), F32), vm((NL, C1), jnp.int32), vm((NL, C1), jnp.int32),
            vm((1, C1), jnp.int32), vm((1, C1), jnp.int32), vm((P2, N2), F32), vm((P2, N2), F32),
            vm((NL, H), jnp.int32), vm((NL, 3 * N2, H), BF16),
            vm((NL, H, B), BF16), vm((NL, H, B), BF16),
            vm((NL, 256, B), BF16), vm((NL, 256, B), BF16), vm((G, H), F32),
            pltpu.SemaphoreType.DMA((10,)), pltpu.SemaphoreType.DMA((10,)),
            pltpu.SemaphoreType.DMA((10,)),
            pltpu.SemaphoreType.DMA((2, 2, NL)), pltpu.SemaphoreType.DMA((2, 2, NL)),
            pltpu.SemaphoreType.DMA((2, 4)), pltpu.SemaphoreType.DMA((2, 4)),
            pltpu.SemaphoreType.DMA((6,)), pltpu.SemaphoreType.DMA((6,)),
        ]
        return pl.pallas_call(
            functools.partial(kernel, S, R, NL, K, C1, P2, N2),
            out_shape=jax.ShapeDtypeStruct(args[0].shape, F32),
            in_specs=[pl.BlockSpec(memory_space=pl.ANY)] * len(args),
            out_specs=pl.BlockSpec(memory_space=pltpu.VMEM),
            scratch_shapes=scratch,
            compiler_params=pltpu.CompilerParams(
                collective_id=0, has_side_effects=True, vmem_limit_bytes=56 * 2**20),
        )(*args[:6], args[6].T, args[7], jnp.transpose(args[8], (1, 0, 2)), args[9].T)

    in_specs = (
        P("sub", "region", None, None),
        P("sub", "region", None, None),
        P("sub", "region", None, None),
        P("sub", "region", None),
        P("sub", "region", None),
        P("sub", "region", None),
        P(),
        P("region", "sub", None),
        P("region", None, None),
        P(None, "region"),
    )
    out_specs = P("sub", "region", None, None)
    return jax.shard_map(
        on_device, mesh=mesh, in_specs=in_specs, out_specs=out_specs, check_vma=False
    )
```

```python
import functools

import jax
import jax.numpy as jnp
from jax import lax
from jax.experimental import pallas as pl
from jax.experimental.pallas import tpu as pltpu
from jax.sharding import PartitionSpec as P

H = 128
EARLY = 3
X = 4
MESH = pl.DeviceIdType.MESH
F32 = jnp.float32
BF16 = jnp.bfloat16


def split(x):
    high = x.astype(BF16)
    return high, (x - high.astype(F32)).astype(BF16)


def nn(a, b):
    return jnp.dot(a, b, preferred_element_type=F32)


def nt(a, b):
    return lax.dot_general(a, b, (((1,), (1,)), ((), ())), preferred_element_type=F32)


def three(product, x, high, low):
    rows = x.shape[0]
    x_high, x_low = split(x)
    both = product(jnp.concatenate([x_high, x_low], axis=0), high)
    return both[:rows] + both[rows:] + product(x_high, low)


def pick(face, order):
    return jnp.take_along_axis(face, jnp.broadcast_to(order, face.shape), axis=1)


def kernel(
    S, R, NL, K, C1, P2, N2,
    pieces, local_inverse, basis, match_south, match_east, primal_index, stiffness,
    level2_inverse, level2_basis, top_inverse,
    out,
    pc, inv, bas, south, east, north_table, west_table, index, stiff, l2inv, l2b, l2pad, topt, topv,
    weight, unsouth, unwest,
    look, lbb_high, lbb_low, lb_stack, t_high, t_low,
    got_west, got_east, got_north, got_south,
    asm, fixed, lhs_two, rows_sent, rows_got, lift_own, lift_got,
    top_sent, top_got, cast_own, cast_got, lhs, fix_own, fix_got, two, tf,
    comb, got_west2, got_east2, got_north2, got_south2,
    weight_near, bas_west, bas_east, bas_north, bas_south, index_west, index_east, index_north,
    index_south, l2_west, l2_east, slots, looks, big_b_high, big_b_low, big_q_high, big_q_low,
    fix_rolled, relay, more_send, more_recv,
    load_sem, edge_send, edge_recv, small_send, small_recv, step_send, step_recv,
):
    s = lax.axis_index("sub")
    b = lax.axis_index("region")
    G = K // S
    OWN = N2 // S
    north_of, south_of = (lax.rem(s + S - 1, S), b), (lax.rem(s + 1, S), b)
    west_of, east_of = (s, lax.rem(b + R - 1, R)), (s, lax.rem(b + 1, R))

    barrier = pltpu.get_barrier_semaphore()

    def tell(region, own=s):
        pl.semaphore_signal(barrier, inc=1, device_id=(own, region), device_id_type=MESH)

    def tell_sub(i, c):
        tell(b, lax.rem(s + i, S))
        return c

    up, down = lax.rem(b + X, R), lax.rem(b + R - X, R)

    def relay_start(k, regions):
        for region in regions:
            pl.semaphore_signal(
                relay.at[k], inc=1, device_id=(s, region), device_id_type=MESH)

    def relay_wait(k):
        pl.semaphore_wait(relay.at[k], 2)

    own_rows = pl.ds(pl.multiple_of(s * OWN, 8), OWN)
    loads = [
        pltpu.make_async_copy(match_east.at[:, 0], east, load_sem.at[0]),
        pltpu.make_async_copy(match_south.at[:, 0], south, load_sem.at[1]),
        pltpu.make_async_copy(pieces.at[:, 0], pc, load_sem.at[2]),
        pltpu.make_async_copy(stiffness, stiff, load_sem.at[3]),
        pltpu.make_async_copy(primal_index.at[:, 0], index, load_sem.at[4]),
        pltpu.make_async_copy(basis.at[:, 0], bas, load_sem.at[5]),
        pltpu.make_async_copy(level2_basis.at[:, 0], l2b, load_sem.at[6]),
        pltpu.make_async_copy(level2_inverse.at[0], l2inv.at[own_rows], load_sem.at[7]),
        pltpu.make_async_copy(top_inverse, topt, load_sem.at[8]),
        pltpu.make_async_copy(local_inverse.at[:, 0], inv, load_sem.at[9]),
    ]
    for region in (east_of[1], west_of[1], up, down):
        tell(region)
    for i in range(1, X):
        tell(b // X * X + lax.rem(b + i, X))
    lax.fori_loop(1, S, tell_sub, 0)
    for load in loads:
        load.start()
    pl.semaphore_wait(barrier, 4 + X - 1 + S - 1)
    relay_start(0, (up, down))
    relay_start(4, (east_of[1], west_of[1]))

    def remote(src, dst, send, recv, device):
        return pltpu.make_async_remote_copy(
            src_ref=src, dst_ref=dst, send_sem=send, recv_sem=recv, device_id=device,
            device_id_type=MESH)

    def edges(phase, face, west_got, east_got, north_got, south_got):
        def to_west(a):
            return remote(face(a, 2), east_got.at[a],
                          edge_send.at[phase, 0, a], edge_recv.at[phase, 0, a], west_of)

        def to_east(a):
            return remote(face(a, 3), west_got.at[a],
                          edge_send.at[phase, 1, a], edge_recv.at[phase, 1, a], east_of)

        to_north = remote(face(0, 0), south_got,
                          small_send.at[phase, 0], small_recv.at[phase, 0], north_of)
        to_south = remote(face(NL - 1, 1), north_got,
                          small_send.at[phase, 1], small_recv.at[phase, 1], south_of)
        return to_west, to_east, to_north, to_south

    to_west, to_east, to_north, to_south = edges(
        0, lambda a, f: pieces.at[a, 0, :, pl.ds(f * H, H)],
        got_west, got_east, got_north, got_south)
    table_east = remote(match_east.at[:, 0], west_table,
                        small_send.at[0, 2], small_recv.at[0, 2], east_of)
    table_south = remote(match_south.at[NL - 1], north_table,
                         small_send.at[0, 3], small_recv.at[0, 3], south_of)
    table_east.start()
    table_south.start()
    for a in range(NL):
        to_west(a).start()
        to_east(a).start()
    to_north.start()
    to_south.start()

    def others(count, me, make):
        def body(i, c):
            make(lax.rem(me + i, count)).start()
            return c
        lax.fori_loop(1, count, body, 0)

    others(S, s, lambda o: remote(
        level2_inverse.at[0], l2inv.at[own_rows], step_send.at[3], step_recv.at[3], (o, b)))

    def face(f):
        return basis.at[:, 0, :, pl.ds(f * H, H)]

    more = [(face(3), bas_west, east_of), (primal_index.at[:, 0], index_west, east_of),
            (level2_basis.at[:, 0], l2_west, east_of),
            (face(2), bas_east, west_of), (primal_index.at[:, 0], index_east, west_of),
            (level2_basis.at[:, 0], l2_east, west_of),
            (basis.at[NL - 1, 0, :, pl.ds(H, H)], bas_north, south_of),
            (primal_index.at[NL - 1], index_north, south_of),
            (basis.at[0, 0, :, pl.ds(0, H)], bas_south, north_of),
            (primal_index.at[0], index_south, north_of)]
    more = [remote(src, dst, more_send.at[i], more_recv.at[i], device)
            for i, (src, dst, device) in enumerate(more)]
    for copy in more:
        copy.start()

    lane = lax.broadcasted_iota(jnp.int32, (K, H), 1).astype(F32).astype(BF16)
    face_row = lax.broadcasted_iota(jnp.int32, (H, H), 0)

    def invert(order):
        hit = (face_row == order).astype(F32).astype(BF16)
        return nt(lane, hit).astype(jnp.int32)

    loads[0].wait()
    loads[1].wait()
    for a in range(NL - 1):
        unsouth[a] = invert(south[a:a + 1, :])

    relay_wait(0)
    relay_start(1, (up, down))

    loads[3].wait()
    levels = stiff[...].astype(F32)
    regions = lax.broadcasted_iota(jnp.int32, levels.shape, 0)
    spots = (lax.broadcasted_iota(jnp.int32, (NL, levels.shape[1]), 1)
             - lax.broadcasted_iota(jnp.int32, (NL, levels.shape[1]), 0) - s * NL)

    def level(region, step):
        row = jnp.sum(jnp.where(regions == region, levels, 0.0), axis=0, keepdims=True)
        return jnp.sum(jnp.where(spots == step, row, 0.0), axis=1, keepdims=True)

    own = level(b, 0)
    for f, other in enumerate((level(b, -1), level(b, 1), level(b - 1, 0), level(b + 1, 0))):
        weight[:, f * H:(f + 1) * H] = jnp.broadcast_to(own / (own + other), (NL, H))
        weight_near[:, f * H:(f + 1) * H] = jnp.broadcast_to(other / (own + other), (NL, H))

    loads[4].wait()
    loads[5].wait()
    loads[6].wait()
    l2pad[...] = jnp.zeros_like(l2pad)
    l2pad[0:P2, :] = l2b[...]
    l2_high, l2_low = split(l2pad[...])
    lb_stack[0:64, :] = l2_high
    lb_stack[64:128, :] = l2_low
    unknown = lax.broadcasted_iota(jnp.int32, (N2, C1), 0)
    odd = lax.rem(b, 2)
    lbb_high[...] = jnp.zeros_like(lbb_high)
    lbb_low[...] = jnp.zeros_like(lbb_low)
    half = pl.ds(pl.multiple_of(odd * 64, 64), 64)
    for a in range(NL):
        hit = (unknown == index[a:a + 1, :]).astype(F32).astype(BF16)
        look[a] = hit
        lb = nn(lb_stack[...], hit)
        lb_high, lb_low = lb[:64].astype(BF16), lb[64:].astype(BF16)
        b_high, b_low = split(bas[a])
        both = nn(jnp.concatenate([lb_high, lb_low], axis=0), b_high)
        lbb = (both[:64] + both[64:] + nn(lb_high, b_low)) * weight[a:a + 1, :]
        high, low = split(lbb)
        lbb_high[half, 4 * H * a:4 * H * (a + 1)] = high
        lbb_low[half, 4 * H * a:4 * H * (a + 1)] = low

    relay_wait(1)
    relay_start(2, (up, down))

    loads[8].wait()
    for c in range(R * P2 // 128):
        topv[128 * c:128 * (c + 1), :] = topt[:, 128 * c:128 * (c + 1)].T
    topv[R * P2:, :] = jnp.zeros_like(topv[R * P2:, :])

    def spread_top(p, c):
        block = topv[pl.ds(pl.multiple_of(2 * P2 * p, 8), 2 * P2 + 8), :]
        pair = jnp.concatenate([block[0:64], block[P2:P2 + 64]], axis=0)
        high, low = split(pair)
        at = pl.ds(pl.multiple_of(128 * p, 128), 128)
        t_high[at, :] = high
        t_low[at, :] = low
        return c

    lax.fori_loop(0, R // 2, spread_top, 0)

    def masked(condition, value):
        return jnp.where(condition, value, jnp.zeros_like(value))

    relay_wait(2)
    relay_start(3, (up, down))

    table_south.wait_recv()
    unsouth[NL - 1] = invert(north_table[...])
    table_east.wait_recv()
    for a in range(NL):
        unwest[a] = invert(west_table[a:a + 1, :])
    loads[2].wait()
    to_north.wait_recv()
    to_south.wait_recv()
    for a in range(NL):
        before = pick(masked(s > 0, got_north[...]) if a == 0 else pc[a - 1, :, H:2 * H],
                      unsouth[(a + NL - 1) % NL])
        after = pick(masked(s < S - 1, got_south[...]) if a == NL - 1 else pc[a + 1, :, 0:H],
                     south[a:a + 1, :])
        at = 4 * H * a
        asm[:, at:at + H] = pc[a, :, 0:H] + before
        asm[:, at + H:at + 2 * H] = pc[a, :, H:2 * H] + after
    top = jnp.zeros((K, H), F32)
    for a in range(NL):
        at = 4 * H * a
        to_east(a).wait_recv()
        asm[:, at + 2 * H:at + 3 * H] = pc[a, :, 2 * H:3 * H] + masked(
            b > 0, pick(got_west[a], unwest[a]))
        to_west(a).wait_recv()
        asm[:, at + 3 * H:at + 4 * H] = pc[a, :, 3 * H:] + masked(
            b < R - 1, pick(got_east[a], east[a:a + 1, :]))
        top += three(nt, asm[:, at:at + 4 * H], lbb_high[:, at:at + 4 * H],
                     lbb_low[:, at:at + 4 * H])

    for g in range(S):
        top_sent[g] = top[G * g:G * (g + 1)]

    def arrived(ref, count, sem):
        pltpu.make_async_copy(ref.at[pl.ds(0, count)], ref.at[pl.ds(0, count)], sem).wait()

    top_got[s] = top_sent[s]
    others(S, s, lambda o: remote(
        top_sent.at[o], top_got.at[s], step_send.at[0], step_recv.at[0], (o, b)))

    two_in = jnp.zeros((K, N2), F32)
    for a in range(NL):
        scaled = asm[:, 4 * H * a:4 * H * (a + 1)] * weight[a:a + 1, :]
        asm[:, 4 * H * a:4 * H * (a + 1)] = scaled
        b_high, b_low = split(bas[a])
        c_high, c_low = split(three(nt, scaled, b_high, b_low))
        both = nt(jnp.concatenate([c_high, c_low], axis=0), look[a])
        two_in += both[:K] + both[K:]
    for g in range(S):
        rows_sent[g] = two_in[G * g:G * (g + 1)]
    rows_got[s] = rows_sent[s]
    others(S, s, lambda o: remote(
        rows_sent.at[o], rows_got.at[s], step_send.at[1], step_recv.at[1], (o, b)))

    to_west2, to_east2, to_north2, to_south2 = edges(
        1, lambda a, f: comb.at[a, :, pl.ds(f * H, H)],
        got_west2, got_east2, got_north2, got_south2)
    loads[9].wait()

    def solve(a, c):
        high, low = split(inv[a])
        at = pl.ds(pl.multiple_of(4 * H * a, 4 * H), 4 * H)
        comb[a] = three(nn, asm[:, at], high, low) * weight[pl.ds(a, 1), :]
        to_west2(a).start()
        to_east2(a).start()
        return c

    lax.fori_loop(0, EARLY, solve, 0)

    arrived(top_got, S - 1, step_recv.at[0])
    mine = top_got[0]
    for g in range(1, S):
        mine += top_got[g]
    cast_own[...] = mine
    cast_got[b] = mine

    relay_wait(3)

    def cast(i, c):
        o = lax.rem(b + R // 2 + i, R)

        remote(cast_own, cast_got.at[b], step_send.at[2], step_recv.at[2], (s, o)).start()
        return c

    lax.fori_loop(0, R // 2, cast, 0)
    lax.fori_loop(R // 2 + 1, R, cast, 0)

    lax.fori_loop(EARLY, NL, solve, 0)
    to_north2.start()
    to_south2.start()

    loads[7].wait()
    arrived(l2inv, (S - 1) * OWN, step_recv.at[3])
    i_high, i_low = split(l2inv[...])
    arrived(rows_got, S - 1, step_recv.at[1])
    two_mine = rows_got[0]
    for g in range(1, S):
        two_mine += rows_got[g]
    high = two_mine.astype(BF16).astype(F32)
    lhs_two[0:G, :] = high
    lhs_two[G:2 * G, :] = two_mine - high
    left = lhs_two[...].astype(BF16)
    first = nn(left, i_high)
    lift4 = first[0:G] + first[G:2 * G] + nn(left, i_low)[0:G]
    relay_wait(4)
    lift_own[...] = lift4
    lift_got[s] = lift4

    def spread(i, src, rolled, got, k):
        o = lax.rem(s + i, S)
        remote(rolled, got.at[S + s], step_send.at[k], step_recv.at[k], (o, east_of[1])).start()
        remote(src, got.at[2 * S + s], step_send.at[k], step_recv.at[k], (o, west_of[1])).start()

    def to_three_regions(src, rolled, got, k):
        def body(i, c):
            spread(i, src, rolled, got, k)
            o = lax.rem(s + i, S)
            remote(src, got.at[s], step_send.at[k], step_recv.at[k], (o, b)).start()
            return c
        lax.fori_loop(1, S, body, 0)
        spread(0, src, rolled, got, k)

    to_three_regions(lift_own, lift_own, lift_got, 4)

    for copy in more:
        copy.wait_recv()
    slots[...] = jnp.full_like(slots, -1)
    slots[:, 0:C1] = index[...]
    slots[0:1, C1:2 * C1] = index_north[...]
    slots[1:NL, C1:2 * C1] = index[0:NL - 1, :]
    slots[0:NL - 1, 2 * C1:3 * C1] = index[1:NL, :]
    slots[NL - 1:NL, 2 * C1:3 * C1] = index_south[...]
    slots[:, 3 * C1:4 * C1] = index_west[...]
    slots[:, 4 * C1:5 * C1] = index_east[...]
    stacks = [lb_stack[...]]
    for level2 in (l2_west, l2_east):
        l2pad[0:P2, :] = level2[...]
        stacks.append(jnp.concatenate(split(l2pad[...]), axis=0))
    spot = lax.broadcasted_iota(jnp.int32, (N2, H), 1)
    unknown = lax.broadcasted_iota(jnp.int32, (N2, H), 0)
    big_q_high[:, 192:256, :] = jnp.zeros_like(big_q_high[:, 192:256, :])
    big_q_low[:, 192:256, :] = jnp.zeros_like(big_q_low[:, 192:256, :])
    gap = jnp.zeros((C1, H), F32)
    for a in range(NL):
        hit = jnp.where(unknown == slots[a:a + 1, :], 1.0, 0.0)
        lb_high, lb_low = [], []
        for j, (low_end, high_end) in enumerate(((0, 3), (3, 4), (4, 5))):
            own_hit = jnp.where((spot >= low_end * C1) & (spot < high_end * C1), hit, 0.0).astype(BF16)
            looks[a, j * N2:(j + 1) * N2, :] = own_hit
            lb = nn(stacks[j], own_hit)
            lb_high.append(lb[0:64])
            lb_low.append(lb[64:128])
        north = bas_north[...] if a == 0 else bas[a - 1, :, H:2 * H]
        north_weight = weight_near[0:1, 0:H] if a == 0 else weight[a - 1:a, H:2 * H]
        after = bas_south[...] if a == NL - 1 else bas[a + 1, :, 0:H]
        after_weight = (weight_near[a:a + 1, H:2 * H] if a == NL - 1
                        else weight[a + 1:a + 2, 0:H])
        faces = [
            pick(north, unsouth[(a + NL - 1) % NL, 0:1, :]) * north_weight,
            pick(after, south[a:a + 1, :]) * after_weight,
            pick(bas_west[a], unwest[a, 0:1, :]) * weight_near[a:a + 1, 2 * H:3 * H],
            pick(bas_east[a], east[a:a + 1, :]) * weight_near[a:a + 1, 3 * H:]]
        rows = [bas[a] * weight[a:a + 1, :]]
        for f in range(4):
            rows.append(jnp.concatenate([gap] * f + [faces[f]] + [gap] * (3 - f), axis=1))
        rows.append(jnp.zeros((H - 5 * C1, 4 * H), F32))
        high, low = split(jnp.concatenate(rows, axis=0))
        big_b_high[a] = high
        big_b_low[a] = low
        q_high = jnp.concatenate(lb_high, axis=0).astype(BF16)
        q_low = jnp.concatenate(lb_low, axis=0).astype(BF16)
        both = nn(jnp.concatenate([q_high, q_low], axis=0), high)
        q_high, q_low = split(both[0:192] + both[192:] + nn(q_high, low))
        big_q_high[a, 0:192, :] = q_high
        big_q_low[a, 0:192, :] = q_low

    arrived(cast_got, R - 1, step_recv.at[2])
    for p in range(R // 2):
        pair = cast_got[2 * p] + cast_got[2 * p + 1]
        high = pair.astype(BF16).astype(F32)
        lhs[0:G, H * p:H * (p + 1)] = high
        lhs[G:2 * G, H * p:H * (p + 1)] = pair - high
    left = lhs[...].astype(BF16)
    first = nn(left, t_high[...])
    fix = first[0:G] + first[G:2 * G] + nn(left, t_low[...])[0:G]
    fix_own[...] = jnp.zeros_like(fix_own)
    fix_own[:, 0:P2] = fix
    fix = fix_own[...]
    fix_rolled[...] = pltpu.roll(fix, 64, 1)
    fix_got[s] = fix
    to_three_regions(fix_own, fix_rolled, fix_got, 5)

    to_north2.wait_recv()
    to_south2.wait_recv()
    for a in range(NL):
        before = pick(masked(s > 0, got_north2[...]) if a == 0 else comb[a - 1, :, H:2 * H],
                      unsouth[(a + NL - 1) % NL])
        after = pick(masked(s < S - 1, got_south2[...]) if a == NL - 1 else comb[a + 1, :, 0:H],
                     south[a:a + 1, :])
        to_east2(a).wait_recv()
        to_west2(a).wait_recv()
        west = masked(b > 0, pick(got_west2[a], unwest[a]))
        east_side = masked(b < R - 1, pick(got_east2[a], east[a:a + 1, :]))
        fixed[:, 4 * H * a:4 * H * (a + 1)] = comb[a] + jnp.concatenate(
            [before, after, west, east_side], axis=1)

    arrived(lift_got, 3 * S - 1, step_recv.at[4])
    for j in range(3):
        for g in range(S):
            two[G * g:G * (g + 1), j * N2:(j + 1) * N2] = lift_got[j * S + g]
    two_both = jnp.concatenate(split(two[...]), axis=0)
    for a in range(NL):
        e = nn(two_both, looks[a])
        at = 4 * H * a
        fixed[:, at:at + 4 * H] += three(nn, e[:K] + e[K:], big_b_high[a], big_b_low[a])

    arrived(fix_got, 3 * S - 1, step_recv.at[5])
    for g in range(S):
        tf[G * g:G * (g + 1), 0:H] = fix_got[g] + fix_got[S + g]
        tf[G * g:G * (g + 1), H:2 * H] = fix_got[2 * S + g]
    f_high, f_low = split(tf[...])
    f_both = jnp.concatenate([f_high, f_low], axis=0)
    for a in range(NL):
        both = nn(f_both, big_q_high[a])
        out[a, 0] = fixed[:, 4 * H * a:4 * H * (a + 1)] + both[:K] + both[K:] + nn(
            f_high, big_q_low[a])

    for first in ((to_west, to_east, to_north, to_south),
                  (to_west2, to_east2, to_north2, to_south2)):
        for a in range(NL):
            first[0](a).wait_send()
            first[1](a).wait_send()
        first[2].wait_send()
        first[3].wait_send()
    for copy in more:
        copy.wait_send()
    table_east.wait_send()
    table_south.wait_send()
    arrived(top_got, S - 1, step_send.at[0])
    arrived(rows_got, S - 1, step_send.at[1])
    arrived(cast_got, R - 1, step_send.at[2])
    arrived(l2inv, (S - 1) * OWN, step_send.at[3])
    arrived(lift_got, 3 * S - 1, step_send.at[4])
    arrived(fix_got, 3 * S - 1, step_send.at[5])


def solution(mesh):
    S, R = mesh.shape["sub"], mesh.shape["region"]

    def on_device(*args):
        NL, _, K, B = args[0].shape
        C1 = args[2].shape[2]
        P2, N2 = args[8].shape[1:]
        NA = args[6].shape[0]
        G = K // S
        vm = pltpu.VMEM
        edge = [vm((NL, K, H), F32), vm((NL, K, H), F32), vm((K, H), F32), vm((K, H), F32)]
        scratch = [
            vm((NL, K, B), F32), vm((NL, B, B), F32), vm((NL, C1, B), F32),
            vm((NL, H), jnp.int32), vm((NL, H), jnp.int32), vm((1, H), jnp.int32),
            vm((NL, H), jnp.int32), vm((NL, C1), jnp.int32), vm((R, NA), jnp.int32), vm((N2, N2), F32), vm((P2, N2), F32), vm((64, N2), F32),
            vm((P2, R * P2), F32), vm((R * P2 + 8, P2), F32), vm((NL, B), F32),
            vm((NL, K, H), jnp.int32), vm((NL, K, H), jnp.int32),
            vm((NL, N2, C1), BF16), vm((128, NL * B), BF16), vm((128, NL * B), BF16),
            vm((128, N2), BF16), vm((64 * R, P2), BF16), vm((64 * R, P2), BF16),
            *edge,
            vm((K, NL * B), F32), vm((K, NL * B), F32),
            vm((2 * G, N2), F32),
            vm((S, G, N2), F32), vm((S, G, N2), F32), vm((G, N2), F32), vm((3 * S, G, N2), F32),
            vm((S, G, H), F32), vm((S, G, H), F32), vm((G, H), F32), vm((R, G, H), F32),
            vm((2 * G, R // 2 * H), F32), vm((G, H), F32), vm((3 * S, G, H), F32),
            vm((K, 3 * N2), F32), vm((K, 2 * H), F32),
            vm((NL, K, B), F32), *edge,
            vm((NL, B), F32), vm((NL, C1, H), F32), vm((NL, C1, H), F32), vm((C1, H), F32),
            vm((C1, H), F32), vm((NL, C1), jnp.int32), vm((NL, C1), jnp.int32),
            vm((1, C1), jnp.int32), vm((1, C1), jnp.int32), vm((P2, N2), F32), vm((P2, N2), F32),
            vm((NL, H), jnp.int32), vm((NL, 3 * N2, H), BF16),
            vm((NL, H, B), BF16), vm((NL, H, B), BF16),
            vm((NL, 256, B), BF16), vm((NL, 256, B), BF16), vm((G, H), F32),
            pltpu.SemaphoreType.REGULAR((5,)),
            pltpu.SemaphoreType.DMA((10,)), pltpu.SemaphoreType.DMA((10,)),
            pltpu.SemaphoreType.DMA((10,)),
            pltpu.SemaphoreType.DMA((2, 2, NL)), pltpu.SemaphoreType.DMA((2, 2, NL)),
            pltpu.SemaphoreType.DMA((2, 4)), pltpu.SemaphoreType.DMA((2, 4)),
            pltpu.SemaphoreType.DMA((6,)), pltpu.SemaphoreType.DMA((6,)),
        ]
        return pl.pallas_call(
            functools.partial(kernel, S, R, NL, K, C1, P2, N2),
            out_shape=jax.ShapeDtypeStruct(args[0].shape, F32),
            in_specs=[pl.BlockSpec(memory_space=pl.ANY)] * len(args),
            out_specs=pl.BlockSpec(memory_space=pltpu.VMEM),
            scratch_shapes=scratch,
            compiler_params=pltpu.CompilerParams(
                collective_id=0, has_side_effects=True, vmem_limit_bytes=56 * 2**20),
        )(*args[:6], args[6].T, args[7], jnp.transpose(args[8], (1, 0, 2)), args[9].T)

    in_specs = (
        P("sub", "region", None, None),
        P("sub", "region", None, None),
        P("sub", "region", None, None),
        P("sub", "region", None),
        P("sub", "region", None),
        P("sub", "region", None),
        P(),
        P("region", "sub", None),
        P("region", None, None),
        P(None, "region"),
    )
    out_specs = P("sub", "region", None, None)
    return jax.shard_map(
        on_device, mesh=mesh, in_specs=in_specs, out_specs=out_specs, check_vma=False
    )
```

```python
import functools

import jax
import jax.numpy as jnp
from jax import lax
from jax.experimental import pallas as pl
from jax.experimental.pallas import tpu as pltpu
from jax.sharding import PartitionSpec as P

H = 128
EARLY = 2
X = 4
MESH = pl.DeviceIdType.MESH
F32 = jnp.float32
BF16 = jnp.bfloat16


def split(x):
    high = x.astype(BF16)
    return high, (x - high.astype(F32)).astype(BF16)


def nn(a, b):
    return jnp.dot(a, b, preferred_element_type=F32)


def nt(a, b):
    return lax.dot_general(a, b, (((1,), (1,)), ((), ())), preferred_element_type=F32)


def three(product, x, high, low):
    rows = x.shape[0]
    x_high, x_low = split(x)
    both = product(jnp.concatenate([x_high, x_low], axis=0), high)
    return both[:rows] + both[rows:] + product(x_high, low)


def pick(face, order):
    return jnp.take_along_axis(face, jnp.broadcast_to(order, face.shape), axis=1)


def kernel(
    S, R, NL, K, C1, P2, N2,
    pieces, local_inverse, basis, match_south, match_east, primal_index, stiffness,
    level2_inverse, level2_basis, top_inverse,
    out,
    pc, inv, bas, south, east, north_table, west_table, index, stiff, l2inv, l2b, l2pad, topt, topv,
    weight, unsouth, unwest,
    look, lbb_high, lbb_low, lb_stack, t_high, t_low,
    got_west, got_east, got_north, got_south,
    asm, fixed, lhs_two, rows_sent, rows_got, lift_own, lift_got,
    top_sent, top_got, cast_own, cast_got, lhs, fix_own, fix_got, two, tf,
    comb, got_west2, got_east2, got_north2, got_south2,
    weight_near, bas_west, bas_east, bas_north, bas_south, index_west, index_east, index_north,
    index_south, l2_west, l2_east, slots, looks, big_b_high, big_b_low, big_q_high, big_q_low,
    fix_rolled, relay, more_send, more_recv,
    load_sem, edge_send, edge_recv, small_send, small_recv, step_send, step_recv,
):
    s = lax.axis_index("sub")
    b = lax.axis_index("region")
    G = K // S
    OWN = N2 // S
    north_of, south_of = (lax.rem(s + S - 1, S), b), (lax.rem(s + 1, S), b)
    west_of, east_of = (s, lax.rem(b + R - 1, R)), (s, lax.rem(b + 1, R))

    barrier = pltpu.get_barrier_semaphore()

    def tell(region, own=s):
        pl.semaphore_signal(barrier, inc=1, device_id=(own, region), device_id_type=MESH)

    def tell_sub(i, c):
        tell(b, lax.rem(s + i, S))
        return c

    up, down = lax.rem(b + X, R), lax.rem(b + R - X, R)

    def relay_start(k, regions):
        for region in regions:
            pl.semaphore_signal(
                relay.at[k], inc=1, device_id=(s, region), device_id_type=MESH)

    def relay_wait(k):
        pl.semaphore_wait(relay.at[k], 2)

    own_rows = pl.ds(pl.multiple_of(s * OWN, 8), OWN)
    loads = [
        pltpu.make_async_copy(match_east.at[:, 0], east, load_sem.at[0]),
        pltpu.make_async_copy(match_south.at[:, 0], south, load_sem.at[1]),
        pltpu.make_async_copy(pieces.at[:, 0], pc, load_sem.at[2]),
        pltpu.make_async_copy(stiffness, stiff, load_sem.at[3]),
        pltpu.make_async_copy(primal_index.at[:, 0], index, load_sem.at[4]),
        pltpu.make_async_copy(basis.at[:, 0], bas, load_sem.at[5]),
        pltpu.make_async_copy(level2_basis.at[:, 0], l2b, load_sem.at[6]),
        pltpu.make_async_copy(level2_inverse.at[0], l2inv.at[own_rows], load_sem.at[7]),
        pltpu.make_async_copy(top_inverse, topt, load_sem.at[8]),
        pltpu.make_async_copy(local_inverse.at[:, 0], inv, load_sem.at[9]),
    ]
    for region in (east_of[1], west_of[1], up, down):
        tell(region)
    for i in range(1, X):
        tell(b // X * X + lax.rem(b + i, X))
    lax.fori_loop(1, S, tell_sub, 0)
    for load in loads:
        load.start()
    pl.semaphore_wait(barrier, 4 + X - 1 + S - 1)
    relay_start(0, (up, down))
    relay_start(4, (east_of[1], west_of[1]))

    def remote(src, dst, send, recv, device):
        return pltpu.make_async_remote_copy(
            src_ref=src, dst_ref=dst, send_sem=send, recv_sem=recv, device_id=device,
            device_id_type=MESH)

    def edges(phase, face, west_got, east_got, north_got, south_got):
        def to_west(a):
            return remote(face(a, 2), east_got.at[a],
                          edge_send.at[phase, 0, a], edge_recv.at[phase, 0, a], west_of)

        def to_east(a):
            return remote(face(a, 3), west_got.at[a],
                          edge_send.at[phase, 1, a], edge_recv.at[phase, 1, a], east_of)

        to_north = remote(face(0, 0), south_got,
                          small_send.at[phase, 0], small_recv.at[phase, 0], north_of)
        to_south = remote(face(NL - 1, 1), north_got,
                          small_send.at[phase, 1], small_recv.at[phase, 1], south_of)
        return to_west, to_east, to_north, to_south

    to_west, to_east, to_north, to_south = edges(
        0, lambda a, f: pieces.at[a, 0, :, pl.ds(f * H, H)],
        got_west, got_east, got_north, got_south)
    table_east = remote(match_east.at[:, 0], west_table,
                        small_send.at[0, 2], small_recv.at[0, 2], east_of)
    table_south = remote(match_south.at[NL - 1], north_table,
                         small_send.at[0, 3], small_recv.at[0, 3], south_of)
    table_east.start()
    table_south.start()
    for a in range(NL):
        to_west(a).start()
        to_east(a).start()
    to_north.start()
    to_south.start()

    def others(count, me, make):
        def body(i, c):
            make(lax.rem(me + i, count)).start()
            return c
        lax.fori_loop(1, count, body, 0)

    others(S, s, lambda o: remote(
        level2_inverse.at[0], l2inv.at[own_rows], step_send.at[3], step_recv.at[3], (o, b)))

    def face(f):
        return basis.at[:, 0, :, pl.ds(f * H, H)]

    more = [(face(3), bas_west, east_of), (primal_index.at[:, 0], index_west, east_of),
            (level2_basis.at[:, 0], l2_west, east_of),
            (face(2), bas_east, west_of), (primal_index.at[:, 0], index_east, west_of),
            (level2_basis.at[:, 0], l2_east, west_of),
            (basis.at[NL - 1, 0, :, pl.ds(H, H)], bas_north, south_of),
            (primal_index.at[NL - 1], index_north, south_of),
            (basis.at[0, 0, :, pl.ds(0, H)], bas_south, north_of),
            (primal_index.at[0], index_south, north_of)]
    more = [remote(src, dst, more_send.at[i], more_recv.at[i], device)
            for i, (src, dst, device) in enumerate(more)]
    for copy in more:
        copy.start()

    lane = lax.broadcasted_iota(jnp.int32, (K, H), 1).astype(F32).astype(BF16)
    face_row = lax.broadcasted_iota(jnp.int32, (H, H), 0)

    def invert(order):
        hit = (face_row == order).astype(F32).astype(BF16)
        return nt(lane, hit).astype(jnp.int32)

    loads[0].wait()
    loads[1].wait()
    for a in range(NL - 1):
        unsouth[a] = invert(south[a:a + 1, :])

    relay_wait(0)
    relay_start(1, (up, down))

    loads[3].wait()
    levels = stiff[...].astype(F32)
    regions = lax.broadcasted_iota(jnp.int32, levels.shape, 0)
    spots = (lax.broadcasted_iota(jnp.int32, (NL, levels.shape[1]), 1)
             - lax.broadcasted_iota(jnp.int32, (NL, levels.shape[1]), 0) - s * NL)

    def level(region, step):
        row = jnp.sum(jnp.where(regions == region, levels, 0.0), axis=0, keepdims=True)
        return jnp.sum(jnp.where(spots == step, row, 0.0), axis=1, keepdims=True)

    own = level(b, 0)
    for f, other in enumerate((level(b, -1), level(b, 1), level(b - 1, 0), level(b + 1, 0))):
        weight[:, f * H:(f + 1) * H] = jnp.broadcast_to(own / (own + other), (NL, H))
        weight_near[:, f * H:(f + 1) * H] = jnp.broadcast_to(other / (own + other), (NL, H))

    loads[4].wait()
    loads[5].wait()
    loads[6].wait()
    l2pad[...] = jnp.zeros_like(l2pad)
    l2pad[0:P2, :] = l2b[...]
    l2_high, l2_low = split(l2pad[...])
    lb_stack[0:64, :] = l2_high
    lb_stack[64:128, :] = l2_low
    unknown = lax.broadcasted_iota(jnp.int32, (N2, C1), 0)
    odd = lax.rem(b, 2)
    lbb_high[...] = jnp.zeros_like(lbb_high)
    lbb_low[...] = jnp.zeros_like(lbb_low)
    half = pl.ds(pl.multiple_of(odd * 64, 64), 64)
    for a in range(NL):
        hit = (unknown == index[a:a + 1, :]).astype(F32).astype(BF16)
        look[a] = hit
        lb = nn(lb_stack[...], hit)
        lb_high, lb_low = lb[:64].astype(BF16), lb[64:].astype(BF16)
        b_high, b_low = split(bas[a])
        both = nn(jnp.concatenate([lb_high, lb_low], axis=0), b_high)
        lbb = (both[:64] + both[64:] + nn(lb_high, b_low)) * weight[a:a + 1, :]
        high, low = split(lbb)
        lbb_high[half, 4 * H * a:4 * H * (a + 1)] = high
        lbb_low[half, 4 * H * a:4 * H * (a + 1)] = low

    relay_wait(1)
    relay_start(2, (up, down))

    loads[8].wait()
    for c in range(R * P2 // 128):
        topv[128 * c:128 * (c + 1), :] = topt[:, 128 * c:128 * (c + 1)].T
    topv[R * P2:, :] = jnp.zeros_like(topv[R * P2:, :])

    def spread_top(p, c):
        block = topv[pl.ds(pl.multiple_of(2 * P2 * p, 8), 2 * P2 + 8), :]
        pair = jnp.concatenate([block[0:64], block[P2:P2 + 64]], axis=0)
        high, low = split(pair)
        at = pl.ds(pl.multiple_of(128 * p, 128), 128)
        t_high[at, :] = high
        t_low[at, :] = low
        return c

    lax.fori_loop(0, R // 2, spread_top, 0)

    def masked(condition, value):
        return jnp.where(condition, value, jnp.zeros_like(value))

    relay_wait(2)
    relay_start(3, (up, down))

    table_south.wait_recv()
    unsouth[NL - 1] = invert(north_table[...])
    table_east.wait_recv()
    for a in range(NL):
        unwest[a] = invert(west_table[a:a + 1, :])
    loads[2].wait()
    to_north.wait_recv()
    to_south.wait_recv()
    for a in range(NL):
        before = pick(masked(s > 0, got_north[...]) if a == 0 else pc[a - 1, :, H:2 * H],
                      unsouth[(a + NL - 1) % NL])
        after = pick(masked(s < S - 1, got_south[...]) if a == NL - 1 else pc[a + 1, :, 0:H],
                     south[a:a + 1, :])
        at = 4 * H * a
        asm[:, at:at + H] = pc[a, :, 0:H] + before
        asm[:, at + H:at + 2 * H] = pc[a, :, H:2 * H] + after
    top = jnp.zeros((K, H), F32)
    for a in range(NL):
        at = 4 * H * a
        to_east(a).wait_recv()
        asm[:, at + 2 * H:at + 3 * H] = pc[a, :, 2 * H:3 * H] + masked(
            b > 0, pick(got_west[a], unwest[a]))
        to_west(a).wait_recv()
        asm[:, at + 3 * H:at + 4 * H] = pc[a, :, 3 * H:] + masked(
            b < R - 1, pick(got_east[a], east[a:a + 1, :]))
        top += three(nt, asm[:, at:at + 4 * H], lbb_high[:, at:at + 4 * H],
                     lbb_low[:, at:at + 4 * H])

    for g in range(S):
        top_sent[g] = top[G * g:G * (g + 1)]

    def arrived(ref, count, sem):
        pltpu.make_async_copy(ref.at[pl.ds(0, count)], ref.at[pl.ds(0, count)], sem).wait()

    top_got[s] = top_sent[s]
    others(S, s, lambda o: remote(
        top_sent.at[o], top_got.at[s], step_send.at[0], step_recv.at[0], (o, b)))

    two_in = jnp.zeros((K, N2), F32)
    for a in range(NL):
        scaled = asm[:, 4 * H * a:4 * H * (a + 1)] * weight[a:a + 1, :]
        asm[:, 4 * H * a:4 * H * (a + 1)] = scaled
        b_high, b_low = split(bas[a])
        c_high, c_low = split(three(nt, scaled, b_high, b_low))
        both = nt(jnp.concatenate([c_high, c_low], axis=0), look[a])
        two_in += both[:K] + both[K:]
    for g in range(S):
        rows_sent[g] = two_in[G * g:G * (g + 1)]
    rows_got[s] = rows_sent[s]
    others(S, s, lambda o: remote(
        rows_sent.at[o], rows_got.at[s], step_send.at[1], step_recv.at[1], (o, b)))

    to_west2, to_east2, to_north2, to_south2 = edges(
        1, lambda a, f: comb.at[a, :, pl.ds(f * H, H)],
        got_west2, got_east2, got_north2, got_south2)
    loads[9].wait()

    def solve(a, c):
        high, low = split(inv[a])
        at = pl.ds(pl.multiple_of(4 * H * a, 4 * H), 4 * H)
        comb[a] = three(nn, asm[:, at], high, low) * weight[pl.ds(a, 1), :]
        to_west2(a).start()
        to_east2(a).start()
        return c

    lax.fori_loop(0, EARLY, solve, 0)

    arrived(top_got, S - 1, step_recv.at[0])
    mine = top_got[0]
    for g in range(1, S):
        mine += top_got[g]
    cast_own[...] = mine
    cast_got[b] = mine

    relay_wait(3)

    def cast(i, c):
        o = lax.rem(b + R // 2 + i, R)

        remote(cast_own, cast_got.at[b], step_send.at[2], step_recv.at[2], (s, o)).start()
        return c

    lax.fori_loop(0, R // 2, cast, 0)
    lax.fori_loop(R // 2 + 1, R, cast, 0)

    lax.fori_loop(EARLY, NL, solve, 0)
    to_north2.start()
    to_south2.start()

    loads[7].wait()
    arrived(l2inv, (S - 1) * OWN, step_recv.at[3])
    i_high, i_low = split(l2inv[...])
    arrived(rows_got, S - 1, step_recv.at[1])
    two_mine = rows_got[0]
    for g in range(1, S):
        two_mine += rows_got[g]
    high = two_mine.astype(BF16).astype(F32)
    lhs_two[0:G, :] = high
    lhs_two[G:2 * G, :] = two_mine - high
    left = lhs_two[...].astype(BF16)
    first = nn(left, i_high)
    lift4 = first[0:G] + first[G:2 * G] + nn(left, i_low)[0:G]
    relay_wait(4)
    lift_own[...] = lift4
    lift_got[s] = lift4

    def spread(i, src, rolled, got, k):
        o = lax.rem(s + i, S)
        remote(rolled, got.at[S + s], step_send.at[k], step_recv.at[k], (o, east_of[1])).start()
        remote(src, got.at[2 * S + s], step_send.at[k], step_recv.at[k], (o, west_of[1])).start()

    def to_three_regions(src, rolled, got, k, k_near):
        def body(i, c):
            spread(i, src, rolled, got, k_near)
            o = lax.rem(s + i, S)
            remote(src, got.at[s], step_send.at[k], step_recv.at[k], (o, b)).start()
            return c
        lax.fori_loop(1, S, body, 0)
        spread(0, src, rolled, got, k_near)

    to_three_regions(lift_own, lift_own, lift_got, 4, 4)

    for copy in more:
        copy.wait_recv()
    slots[...] = jnp.full_like(slots, -1)
    slots[:, 0:C1] = index[...]
    slots[0:1, C1:2 * C1] = index_north[...]
    slots[1:NL, C1:2 * C1] = index[0:NL - 1, :]
    slots[0:NL - 1, 2 * C1:3 * C1] = index[1:NL, :]
    slots[NL - 1:NL, 2 * C1:3 * C1] = index_south[...]
    slots[:, 3 * C1:4 * C1] = index_west[...]
    slots[:, 4 * C1:5 * C1] = index_east[...]
    stacks = [lb_stack[...]]
    for level2 in (l2_west, l2_east):
        l2pad[0:P2, :] = level2[...]
        stacks.append(jnp.concatenate(split(l2pad[...]), axis=0))
    spot = lax.broadcasted_iota(jnp.int32, (N2, H), 1)
    unknown = lax.broadcasted_iota(jnp.int32, (N2, H), 0)
    big_q_high[:, 192:256, :] = jnp.zeros_like(big_q_high[:, 192:256, :])
    big_q_low[:, 192:256, :] = jnp.zeros_like(big_q_low[:, 192:256, :])
    gap = jnp.zeros((C1, H), F32)
    for a in range(NL):
        hit = jnp.where(unknown == slots[a:a + 1, :], 1.0, 0.0)
        lb_high, lb_low = [], []
        for j, (low_end, high_end) in enumerate(((0, 3), (3, 4), (4, 5))):
            own_hit = jnp.where((spot >= low_end * C1) & (spot < high_end * C1), hit, 0.0).astype(BF16)
            looks[a, j * N2:(j + 1) * N2, :] = own_hit
            lb = nn(stacks[j], own_hit)
            lb_high.append(lb[0:64])
            lb_low.append(lb[64:128])
        north = bas_north[...] if a == 0 else bas[a - 1, :, H:2 * H]
        north_weight = weight_near[0:1, 0:H] if a == 0 else weight[a - 1:a, H:2 * H]
        after = bas_south[...] if a == NL - 1 else bas[a + 1, :, 0:H]
        after_weight = (weight_near[a:a + 1, H:2 * H] if a == NL - 1
                        else weight[a + 1:a + 2, 0:H])
        faces = [
            pick(north, unsouth[(a + NL - 1) % NL, 0:1, :]) * north_weight,
            pick(after, south[a:a + 1, :]) * after_weight,
            pick(bas_west[a], unwest[a, 0:1, :]) * weight_near[a:a + 1, 2 * H:3 * H],
            pick(bas_east[a], east[a:a + 1, :]) * weight_near[a:a + 1, 3 * H:]]
        rows = [bas[a] * weight[a:a + 1, :]]
        for f in range(4):
            rows.append(jnp.concatenate([gap] * f + [faces[f]] + [gap] * (3 - f), axis=1))
        rows.append(jnp.zeros((H - 5 * C1, 4 * H), F32))
        high, low = split(jnp.concatenate(rows, axis=0))
        big_b_high[a] = high
        big_b_low[a] = low
        q_high = jnp.concatenate(lb_high, axis=0).astype(BF16)
        q_low = jnp.concatenate(lb_low, axis=0).astype(BF16)
        both = nn(jnp.concatenate([q_high, q_low], axis=0), high)
        q_high, q_low = split(both[0:192] + both[192:] + nn(q_high, low))
        big_q_high[a, 0:192, :] = q_high
        big_q_low[a, 0:192, :] = q_low

    arrived(cast_got, R - 1, step_recv.at[2])
    for p in range(R // 2):
        pair = cast_got[2 * p] + cast_got[2 * p + 1]
        high = pair.astype(BF16).astype(F32)
        lhs[0:G, H * p:H * (p + 1)] = high
        lhs[G:2 * G, H * p:H * (p + 1)] = pair - high
    left = lhs[...].astype(BF16)
    first = nn(left, t_high[...])
    fix = first[0:G] + first[G:2 * G] + nn(left, t_low[...])[0:G]
    fix_own[...] = jnp.zeros_like(fix_own)
    fix_own[:, 0:P2] = fix
    fix = fix_own[...]
    fix_rolled[...] = pltpu.roll(fix, 64, 1)
    fix_got[s] = fix
    to_three_regions(fix_own, fix_rolled, fix_got, 5, 6)

    to_north2.wait_recv()
    to_south2.wait_recv()
    for a in range(NL):
        before = pick(masked(s > 0, got_north2[...]) if a == 0 else comb[a - 1, :, H:2 * H],
                      unsouth[(a + NL - 1) % NL])
        after = pick(masked(s < S - 1, got_south2[...]) if a == NL - 1 else comb[a + 1, :, 0:H],
                     south[a:a + 1, :])
        to_east2(a).wait_recv()
        to_west2(a).wait_recv()
        west = masked(b > 0, pick(got_west2[a], unwest[a]))
        east_side = masked(b < R - 1, pick(got_east2[a], east[a:a + 1, :]))
        fixed[:, 4 * H * a:4 * H * (a + 1)] = comb[a] + jnp.concatenate(
            [before, after, west, east_side], axis=1)

    arrived(lift_got, 3 * S - 1, step_recv.at[4])
    for j in range(3):
        for g in range(S):
            two[G * g:G * (g + 1), j * N2:(j + 1) * N2] = lift_got[j * S + g]
    two_both = jnp.concatenate(split(two[...]), axis=0)
    for a in range(NL):
        e = nn(two_both, looks[a])
        at = 4 * H * a
        fixed[:, at:at + 4 * H] += three(nn, e[:K] + e[K:], big_b_high[a], big_b_low[a])

    arrived(fix_got, S - 1, step_recv.at[5])
    for g in range(S):
        tf[G * g:G * (g + 1), 0:H] = fix_got[g]
    f_high, f_low = split(tf[:, 0:H])
    f_both = jnp.concatenate([f_high, f_low], axis=0)
    for a in range(NL):
        both = nn(f_both, big_q_high[a, 0:H, :])
        value = fixed[:, 4 * H * a:4 * H * (a + 1)] + both[:K] + both[K:] + nn(
            f_high, big_q_low[a, 0:H, :])
        out[a, 0, :, 0:2 * H] = value[:, 0:2 * H]
        fixed[:, 4 * H * a + 2 * H:4 * H * (a + 1)] = value[:, 2 * H:]

    arrived(fix_got, 2 * S, step_recv.at[6])
    for g in range(S):
        tf[G * g:G * (g + 1), 0:H] = fix_got[S + g]
        tf[G * g:G * (g + 1), H:2 * H] = fix_got[2 * S + g]
    f_high, f_low = split(tf[...])
    f_both = jnp.concatenate([f_high, f_low], axis=0)
    for a in range(NL):
        both = nn(f_both, big_q_high[a, :, 2 * H:])
        out[a, 0, :, 2 * H:] = fixed[:, 4 * H * a + 2 * H:4 * H * (a + 1)] + both[:K] + both[
            K:] + nn(f_high, big_q_low[a, :, 2 * H:])

    for first in ((to_west, to_east, to_north, to_south),
                  (to_west2, to_east2, to_north2, to_south2)):
        for a in range(NL):
            first[0](a).wait_send()
            first[1](a).wait_send()
        first[2].wait_send()
        first[3].wait_send()
    for copy in more:
        copy.wait_send()
    table_east.wait_send()
    table_south.wait_send()
    arrived(top_got, S - 1, step_send.at[0])
    arrived(rows_got, S - 1, step_send.at[1])
    arrived(cast_got, R - 1, step_send.at[2])
    arrived(l2inv, (S - 1) * OWN, step_send.at[3])
    arrived(lift_got, 3 * S - 1, step_send.at[4])
    arrived(fix_got, S - 1, step_send.at[5])
    arrived(fix_got, 2 * S, step_send.at[6])


def solution(mesh):
    S, R = mesh.shape["sub"], mesh.shape["region"]

    def on_device(*args):
        NL, _, K, B = args[0].shape
        C1 = args[2].shape[2]
        P2, N2 = args[8].shape[1:]
        NA = args[6].shape[0]
        G = K // S
        vm = pltpu.VMEM
        edge = [vm((NL, K, H), F32), vm((NL, K, H), F32), vm((K, H), F32), vm((K, H), F32)]
        scratch = [
            vm((NL, K, B), F32), vm((NL, B, B), F32), vm((NL, C1, B), F32),
            vm((NL, H), jnp.int32), vm((NL, H), jnp.int32), vm((1, H), jnp.int32),
            vm((NL, H), jnp.int32), vm((NL, C1), jnp.int32), vm((R, NA), jnp.int32), vm((N2, N2), F32), vm((P2, N2), F32), vm((64, N2), F32),
            vm((P2, R * P2), F32), vm((R * P2 + 8, P2), F32), vm((NL, B), F32),
            vm((NL, K, H), jnp.int32), vm((NL, K, H), jnp.int32),
            vm((NL, N2, C1), BF16), vm((128, NL * B), BF16), vm((128, NL * B), BF16),
            vm((128, N2), BF16), vm((64 * R, P2), BF16), vm((64 * R, P2), BF16),
            *edge,
            vm((K, NL * B), F32), vm((K, NL * B), F32),
            vm((2 * G, N2), F32),
            vm((S, G, N2), F32), vm((S, G, N2), F32), vm((G, N2), F32), vm((3 * S, G, N2), F32),
            vm((S, G, H), F32), vm((S, G, H), F32), vm((G, H), F32), vm((R, G, H), F32),
            vm((2 * G, R // 2 * H), F32), vm((G, H), F32), vm((3 * S, G, H), F32),
            vm((K, 3 * N2), F32), vm((K, 2 * H), F32),
            vm((NL, K, B), F32), *edge,
            vm((NL, B), F32), vm((NL, C1, H), F32), vm((NL, C1, H), F32), vm((C1, H), F32),
            vm((C1, H), F32), vm((NL, C1), jnp.int32), vm((NL, C1), jnp.int32),
            vm((1, C1), jnp.int32), vm((1, C1), jnp.int32), vm((P2, N2), F32), vm((P2, N2), F32),
            vm((NL, H), jnp.int32), vm((NL, 3 * N2, H), BF16),
            vm((NL, H, B), BF16), vm((NL, H, B), BF16),
            vm((NL, 256, B), BF16), vm((NL, 256, B), BF16), vm((G, H), F32),
            pltpu.SemaphoreType.REGULAR((5,)),
            pltpu.SemaphoreType.DMA((10,)), pltpu.SemaphoreType.DMA((10,)),
            pltpu.SemaphoreType.DMA((10,)),
            pltpu.SemaphoreType.DMA((2, 2, NL)), pltpu.SemaphoreType.DMA((2, 2, NL)),
            pltpu.SemaphoreType.DMA((2, 4)), pltpu.SemaphoreType.DMA((2, 4)),
            pltpu.SemaphoreType.DMA((7,)), pltpu.SemaphoreType.DMA((7,)),
        ]
        return pl.pallas_call(
            functools.partial(kernel, S, R, NL, K, C1, P2, N2),
            out_shape=jax.ShapeDtypeStruct(args[0].shape, F32),
            in_specs=[pl.BlockSpec(memory_space=pl.ANY)] * len(args),
            out_specs=pl.BlockSpec(memory_space=pltpu.VMEM),
            scratch_shapes=scratch,
            compiler_params=pltpu.CompilerParams(
                collective_id=0, has_side_effects=True, vmem_limit_bytes=56 * 2**20),
        )(*args[:6], args[6].T, args[7], jnp.transpose(args[8], (1, 0, 2)), args[9].T)

    in_specs = (
        P("sub", "region", None, None),
        P("sub", "region", None, None),
        P("sub", "region", None, None),
        P("sub", "region", None),
        P("sub", "region", None),
        P("sub", "region", None),
        P(),
        P("region", "sub", None),
        P("region", None, None),
        P(None, "region"),
    )
    out_specs = P("sub", "region", None, None)
    return jax.shard_map(
        on_device, mesh=mesh, in_specs=in_specs, out_specs=out_specs, check_vma=False
    )
```

```python
import functools

import jax
import jax.numpy as jnp
from jax import lax
from jax.experimental import pallas as pl
from jax.experimental.pallas import tpu as pltpu
from jax.sharding import PartitionSpec as P

H = 128
EARLY = 2
X = 4
MESH = pl.DeviceIdType.MESH
F32 = jnp.float32
BF16 = jnp.bfloat16


def split(x):
    high = x.astype(BF16)
    return high, (x - high.astype(F32)).astype(BF16)


def nn(a, b):
    return jnp.dot(a, b, preferred_element_type=F32)


def nt(a, b):
    return lax.dot_general(a, b, (((1,), (1,)), ((), ())), preferred_element_type=F32)


def three(product, x, high, low):
    rows = x.shape[0]
    x_high, x_low = split(x)
    both = product(jnp.concatenate([x_high, x_low], axis=0), high)
    return both[:rows] + both[rows:] + product(x_high, low)


def pick(face, order):
    return jnp.take_along_axis(face, jnp.broadcast_to(order, face.shape), axis=1)


def kernel(
    S, R, NL, K, C1, P2, N2,
    pieces, local_inverse, basis, match_south, match_east, primal_index, stiffness,
    level2_inverse, level2_basis, top_inverse,
    out,
    pc, inv, bas, south, east, north_table, west_table, index, stiff, l2inv, l2b, l2pad, topt, topv,
    weight, unsouth, unwest,
    look, lbb_high, lbb_low, lb_stack, t_high, t_low,
    got_west, got_east, got_north, got_south,
    asm, fixed, lhs_two, rows_sent, rows_got, lift_own, lift_got,
    top_sent, top_got, cast_own, cast_got, lhs, fix_own, fix_got, two, tf,
    comb, got_west2, got_east2, got_north2, got_south2,
    weight_near, bas_west, bas_east, bas_north, bas_south, index_west, index_east, index_north,
    index_south, l2_west, l2_east, slots, looks, big_b_high, big_b_low, big_q_high, big_q_low,
    fix_rolled, relay, more_send, more_recv,
    load_sem, edge_send, edge_recv, small_send, small_recv, step_send, step_recv,
):
    s = lax.axis_index("sub")
    b = lax.axis_index("region")
    G = K // S
    OWN = N2 // S
    north_of, south_of = (lax.rem(s + S - 1, S), b), (lax.rem(s + 1, S), b)
    west_of, east_of = (s, lax.rem(b + R - 1, R)), (s, lax.rem(b + 1, R))

    barrier = pltpu.get_barrier_semaphore()

    def tell(region, own=s):
        pl.semaphore_signal(barrier, inc=1, device_id=(own, region), device_id_type=MESH)

    def tell_sub(i, c):
        tell(b, lax.rem(s + i, S))
        return c

    up, down = lax.rem(b + X, R), lax.rem(b + R - X, R)

    def relay_start(k, regions):
        for region in regions:
            pl.semaphore_signal(
                relay.at[k], inc=1, device_id=(s, region), device_id_type=MESH)

    def relay_wait(k):
        pl.semaphore_wait(relay.at[k], 2)

    own_rows = pl.ds(pl.multiple_of(s * OWN, 8), OWN)
    loads = [
        pltpu.make_async_copy(match_east.at[:, 0], east, load_sem.at[0]),
        pltpu.make_async_copy(match_south.at[:, 0], south, load_sem.at[1]),
        pltpu.make_async_copy(pieces.at[:, 0], pc, load_sem.at[2]),
        pltpu.make_async_copy(stiffness, stiff, load_sem.at[3]),
        pltpu.make_async_copy(primal_index.at[:, 0], index, load_sem.at[4]),
        pltpu.make_async_copy(basis.at[:, 0], bas, load_sem.at[5]),
        pltpu.make_async_copy(level2_basis.at[:, 0], l2b, load_sem.at[6]),
        pltpu.make_async_copy(level2_inverse.at[0], l2inv.at[own_rows], load_sem.at[7]),
        pltpu.make_async_copy(top_inverse, topt, load_sem.at[8]),
        pltpu.make_async_copy(local_inverse.at[:, 0], inv, load_sem.at[9]),
    ]
    for region in (east_of[1], west_of[1], up, down):
        tell(region)
    for i in range(1, X):
        tell(b // X * X + lax.rem(b + i, X))
    lax.fori_loop(1, S, tell_sub, 0)
    for load in loads:
        load.start()
    pl.semaphore_wait(barrier, 4 + X - 1 + S - 1)
    relay_start(0, (up, down))
    relay_start(4, (east_of[1], west_of[1]))

    def remote(src, dst, send, recv, device):
        return pltpu.make_async_remote_copy(
            src_ref=src, dst_ref=dst, send_sem=send, recv_sem=recv, device_id=device,
            device_id_type=MESH)

    def edges(phase, face, west_got, east_got, north_got, south_got):
        def to_west(a):
            return remote(face(a, 2), east_got.at[a],
                          edge_send.at[phase, 0, a], edge_recv.at[phase, 0, a], west_of)

        def to_east(a):
            return remote(face(a, 3), west_got.at[a],
                          edge_send.at[phase, 1, a], edge_recv.at[phase, 1, a], east_of)

        to_north = remote(face(0, 0), south_got,
                          small_send.at[phase, 0], small_recv.at[phase, 0], north_of)
        to_south = remote(face(NL - 1, 1), north_got,
                          small_send.at[phase, 1], small_recv.at[phase, 1], south_of)
        return to_west, to_east, to_north, to_south

    to_west, to_east, to_north, to_south = edges(
        0, lambda a, f: pieces.at[a, 0, :, pl.ds(f * H, H)],
        got_west, got_east, got_north, got_south)
    table_east = remote(match_east.at[:, 0], west_table,
                        small_send.at[0, 2], small_recv.at[0, 2], east_of)
    table_south = remote(match_south.at[NL - 1], north_table,
                         small_send.at[0, 3], small_recv.at[0, 3], south_of)
    table_east.start()
    table_south.start()
    for a in range(NL):
        to_west(a).start()
        to_east(a).start()
    to_north.start()
    to_south.start()

    def others(count, me, make):
        def body(i, c):
            make(lax.rem(me + i, count)).start()
            return c
        lax.fori_loop(1, count, body, 0)

    others(S, s, lambda o: remote(
        level2_inverse.at[0], l2inv.at[own_rows], step_send.at[3], step_recv.at[3], (o, b)))

    def face(f):
        return basis.at[:, 0, :, pl.ds(f * H, H)]

    more = [(face(3), bas_west, east_of), (primal_index.at[:, 0], index_west, east_of),
            (level2_basis.at[:, 0], l2_west, east_of),
            (face(2), bas_east, west_of), (primal_index.at[:, 0], index_east, west_of),
            (level2_basis.at[:, 0], l2_east, west_of),
            (basis.at[NL - 1, 0, :, pl.ds(H, H)], bas_north, south_of),
            (primal_index.at[NL - 1], index_north, south_of),
            (basis.at[0, 0, :, pl.ds(0, H)], bas_south, north_of),
            (primal_index.at[0], index_south, north_of)]
    more = [remote(src, dst, more_send.at[i], more_recv.at[i], device)
            for i, (src, dst, device) in enumerate(more)]
    for copy in more:
        copy.start()

    lane = lax.broadcasted_iota(jnp.int32, (K, H), 1).astype(F32).astype(BF16)
    face_row = lax.broadcasted_iota(jnp.int32, (H, H), 0)

    def invert(order):
        hit = (face_row == order).astype(F32).astype(BF16)
        return nt(lane, hit).astype(jnp.int32)

    loads[0].wait()
    loads[1].wait()
    for a in range(NL - 1):
        unsouth[a] = invert(south[a:a + 1, :])

    relay_wait(0)
    relay_start(1, (up, down))

    loads[3].wait()
    levels = stiff[...].astype(F32)
    regions = lax.broadcasted_iota(jnp.int32, levels.shape, 0)
    spots = (lax.broadcasted_iota(jnp.int32, (NL, levels.shape[1]), 1)
             - lax.broadcasted_iota(jnp.int32, (NL, levels.shape[1]), 0) - s * NL)

    def level(region, step):
        row = jnp.sum(jnp.where(regions == region, levels, 0.0), axis=0, keepdims=True)
        return jnp.sum(jnp.where(spots == step, row, 0.0), axis=1, keepdims=True)

    own = level(b, 0)
    for f, other in enumerate((level(b, -1), level(b, 1), level(b - 1, 0), level(b + 1, 0))):
        weight[:, f * H:(f + 1) * H] = jnp.broadcast_to(own / (own + other), (NL, H))
        weight_near[:, f * H:(f + 1) * H] = jnp.broadcast_to(other / (own + other), (NL, H))

    loads[4].wait()
    loads[5].wait()
    loads[6].wait()
    l2pad[...] = jnp.zeros_like(l2pad)
    l2pad[0:P2, :] = l2b[...]
    l2_high, l2_low = split(l2pad[...])
    lb_stack[0:64, :] = l2_high
    lb_stack[64:128, :] = l2_low
    unknown = lax.broadcasted_iota(jnp.int32, (N2, C1), 0)
    odd = lax.rem(b, 2)
    lbb_high[...] = jnp.zeros_like(lbb_high)
    lbb_low[...] = jnp.zeros_like(lbb_low)
    half = pl.ds(pl.multiple_of(odd * 64, 64), 64)
    for a in range(NL):
        hit = (unknown == index[a:a + 1, :]).astype(F32).astype(BF16)
        look[a] = hit
        lb = nn(lb_stack[...], hit)
        lb_high, lb_low = lb[:64].astype(BF16), lb[64:].astype(BF16)
        b_high, b_low = split(bas[a])
        both = nn(jnp.concatenate([lb_high, lb_low], axis=0), b_high)
        lbb = (both[:64] + both[64:] + nn(lb_high, b_low)) * weight[a:a + 1, :]
        high, low = split(lbb)
        lbb_high[half, 4 * H * a:4 * H * (a + 1)] = high
        lbb_low[half, 4 * H * a:4 * H * (a + 1)] = low

    relay_wait(1)
    relay_start(2, (up, down))

    loads[8].wait()
    for c in range(R * P2 // 128):
        topv[128 * c:128 * (c + 1), :] = topt[:, 128 * c:128 * (c + 1)].T
    topv[R * P2:, :] = jnp.zeros_like(topv[R * P2:, :])

    def spread_top(p, c):
        block = topv[pl.ds(pl.multiple_of(2 * P2 * p, 8), 2 * P2 + 8), :]
        pair = jnp.concatenate([block[0:64], block[P2:P2 + 64]], axis=0)
        high, low = split(pair)
        at = pl.ds(pl.multiple_of(128 * p, 128), 128)
        t_high[at, :] = high
        t_low[at, :] = low
        return c

    lax.fori_loop(0, R // 2, spread_top, 0)

    def masked(condition, value):
        return jnp.where(condition, value, jnp.zeros_like(value))

    relay_wait(2)
    relay_start(3, (up, down))

    table_south.wait_recv()
    unsouth[NL - 1] = invert(north_table[...])
    table_east.wait_recv()
    for a in range(NL):
        unwest[a] = invert(west_table[a:a + 1, :])
    loads[2].wait()
    to_north.wait_recv()
    to_south.wait_recv()
    for a in range(NL):
        before = pick(masked(s > 0, got_north[...]) if a == 0 else pc[a - 1, :, H:2 * H],
                      unsouth[(a + NL - 1) % NL])
        after = pick(masked(s < S - 1, got_south[...]) if a == NL - 1 else pc[a + 1, :, 0:H],
                     south[a:a + 1, :])
        at = 4 * H * a
        asm[:, at:at + H] = pc[a, :, 0:H] + before
        asm[:, at + H:at + 2 * H] = pc[a, :, H:2 * H] + after
    top = jnp.zeros((K, H), F32)
    for a in range(NL):
        at = 4 * H * a
        to_east(a).wait_recv()
        asm[:, at + 2 * H:at + 3 * H] = pc[a, :, 2 * H:3 * H] + masked(
            b > 0, pick(got_west[a], unwest[a]))
        to_west(a).wait_recv()
        asm[:, at + 3 * H:at + 4 * H] = pc[a, :, 3 * H:] + masked(
            b < R - 1, pick(got_east[a], east[a:a + 1, :]))
        top += three(nt, asm[:, at:at + 4 * H], lbb_high[:, at:at + 4 * H],
                     lbb_low[:, at:at + 4 * H])

    for g in range(S):
        top_sent[g] = top[G * g:G * (g + 1)]

    def arrived(ref, count, sem):
        pltpu.make_async_copy(ref.at[pl.ds(0, count)], ref.at[pl.ds(0, count)], sem).wait()

    top_got[s] = top_sent[s]
    others(S, s, lambda o: remote(
        top_sent.at[o], top_got.at[s], step_send.at[0], step_recv.at[0], (o, b)))

    two_in = jnp.zeros((K, N2), F32)
    for a in range(NL):
        scaled = asm[:, 4 * H * a:4 * H * (a + 1)] * weight[a:a + 1, :]
        asm[:, 4 * H * a:4 * H * (a + 1)] = scaled
        b_high, b_low = split(bas[a])
        c_high, c_low = split(three(nt, scaled, b_high, b_low))
        both = nt(jnp.concatenate([c_high, c_low], axis=0), look[a])
        two_in += both[:K] + both[K:]
    for g in range(S):
        rows_sent[g] = two_in[G * g:G * (g + 1)]
    rows_got[s] = rows_sent[s]
    others(S, s, lambda o: remote(
        rows_sent.at[o], rows_got.at[s], step_send.at[1], step_recv.at[1], (o, b)))

    to_west2, to_east2, to_north2, to_south2 = edges(
        1, lambda a, f: comb.at[a, :, pl.ds(f * H, H)],
        got_west2, got_east2, got_north2, got_south2)
    loads[9].wait()

    def solve(a, c):
        high, low = split(inv[a])
        at = pl.ds(pl.multiple_of(4 * H * a, 4 * H), 4 * H)
        comb[a] = three(nn, asm[:, at], high, low) * weight[pl.ds(a, 1), :]
        to_west2(a).start()
        to_east2(a).start()
        return c

    lax.fori_loop(0, EARLY, solve, 0)

    arrived(top_got, S - 1, step_recv.at[0])
    mine = top_got[0]
    for g in range(1, S):
        mine += top_got[g]
    cast_own[...] = mine
    cast_got[b] = mine

    relay_wait(3)

    def cast(i, c):
        o = lax.rem(b + i, R)
        remote(cast_own, cast_got.at[b], step_send.at[2], step_recv.at[2], (s, o)).start()
        return c

    for i in sorted(range(1, R), key=lambda i: (abs(R // 2 - i), i)):
        cast(i, 0)

    lax.fori_loop(EARLY, NL, solve, 0)
    to_north2.start()
    to_south2.start()

    loads[7].wait()
    arrived(l2inv, (S - 1) * OWN, step_recv.at[3])
    i_high, i_low = split(l2inv[...])
    arrived(rows_got, S - 1, step_recv.at[1])
    two_mine = rows_got[0]
    for g in range(1, S):
        two_mine += rows_got[g]
    high = two_mine.astype(BF16).astype(F32)
    lhs_two[0:G, :] = high
    lhs_two[G:2 * G, :] = two_mine - high
    left = lhs_two[...].astype(BF16)
    first = nn(left, i_high)
    lift4 = first[0:G] + first[G:2 * G] + nn(left, i_low)[0:G]
    relay_wait(4)
    lift_own[...] = lift4
    lift_got[s] = lift4

    def spread(i, src, rolled, got, k):
        o = lax.rem(s + i, S)
        remote(rolled, got.at[S + s], step_send.at[k], step_recv.at[k], (o, east_of[1])).start()
        remote(src, got.at[2 * S + s], step_send.at[k], step_recv.at[k], (o, west_of[1])).start()

    def to_three_regions(src, rolled, got, k, k_near):
        def body(i, c):
            spread(i, src, rolled, got, k_near)
            o = lax.rem(s + i, S)
            remote(src, got.at[s], step_send.at[k], step_recv.at[k], (o, b)).start()
            return c
        for i in sorted(range(1, S), key=lambda i: (abs(S // 2 - i), i)):
            body(i, 0)
        spread(0, src, rolled, got, k_near)

    to_three_regions(lift_own, lift_own, lift_got, 4, 4)

    for copy in more:
        copy.wait_recv()
    slots[...] = jnp.full_like(slots, -1)
    slots[:, 0:C1] = index[...]
    slots[0:1, C1:2 * C1] = index_north[...]
    slots[1:NL, C1:2 * C1] = index[0:NL - 1, :]
    slots[0:NL - 1, 2 * C1:3 * C1] = index[1:NL, :]
    slots[NL - 1:NL, 2 * C1:3 * C1] = index_south[...]
    slots[:, 3 * C1:4 * C1] = index_west[...]
    slots[:, 4 * C1:5 * C1] = index_east[...]
    stacks = [lb_stack[...]]
    for level2 in (l2_west, l2_east):
        l2pad[0:P2, :] = level2[...]
        stacks.append(jnp.concatenate(split(l2pad[...]), axis=0))
    spot = lax.broadcasted_iota(jnp.int32, (N2, H), 1)
    unknown = lax.broadcasted_iota(jnp.int32, (N2, H), 0)
    big_q_high[:, 192:256, :] = jnp.zeros_like(big_q_high[:, 192:256, :])
    big_q_low[:, 192:256, :] = jnp.zeros_like(big_q_low[:, 192:256, :])
    gap = jnp.zeros((C1, H), F32)
    for a in range(NL):
        hit = jnp.where(unknown == slots[a:a + 1, :], 1.0, 0.0)
        lb_high, lb_low = [], []
        for j, (low_end, high_end) in enumerate(((0, 3), (3, 4), (4, 5))):
            own_hit = jnp.where((spot >= low_end * C1) & (spot < high_end * C1), hit, 0.0).astype(BF16)
            looks[a, j * N2:(j + 1) * N2, :] = own_hit
            lb = nn(stacks[j], own_hit)
            lb_high.append(lb[0:64])
            lb_low.append(lb[64:128])
        north = bas_north[...] if a == 0 else bas[a - 1, :, H:2 * H]
        north_weight = weight_near[0:1, 0:H] if a == 0 else weight[a - 1:a, H:2 * H]
        after = bas_south[...] if a == NL - 1 else bas[a + 1, :, 0:H]
        after_weight = (weight_near[a:a + 1, H:2 * H] if a == NL - 1
                        else weight[a + 1:a + 2, 0:H])
        faces = [
            pick(north, unsouth[(a + NL - 1) % NL, 0:1, :]) * north_weight,
            pick(after, south[a:a + 1, :]) * after_weight,
            pick(bas_west[a], unwest[a, 0:1, :]) * weight_near[a:a + 1, 2 * H:3 * H],
            pick(bas_east[a], east[a:a + 1, :]) * weight_near[a:a + 1, 3 * H:]]
        rows = [bas[a] * weight[a:a + 1, :]]
        for f in range(4):
            rows.append(jnp.concatenate([gap] * f + [faces[f]] + [gap] * (3 - f), axis=1))
        rows.append(jnp.zeros((H - 5 * C1, 4 * H), F32))
        high, low = split(jnp.concatenate(rows, axis=0))
        big_b_high[a] = high
        big_b_low[a] = low
        q_high = jnp.concatenate(lb_high, axis=0).astype(BF16)
        q_low = jnp.concatenate(lb_low, axis=0).astype(BF16)
        both = nn(jnp.concatenate([q_high, q_low], axis=0), high)
        q_high, q_low = split(both[0:192] + both[192:] + nn(q_high, low))
        big_q_high[a, 0:192, :] = q_high
        big_q_low[a, 0:192, :] = q_low

    arrived(cast_got, R - 1, step_recv.at[2])
    for p in range(R // 2):
        pair = cast_got[2 * p] + cast_got[2 * p + 1]
        high = pair.astype(BF16).astype(F32)
        lhs[0:G, H * p:H * (p + 1)] = high
        lhs[G:2 * G, H * p:H * (p + 1)] = pair - high
    left = lhs[...].astype(BF16)
    first = nn(left, t_high[...])
    fix = first[0:G] + first[G:2 * G] + nn(left, t_low[...])[0:G]
    fix_own[...] = jnp.zeros_like(fix_own)
    fix_own[:, 0:P2] = fix
    fix = fix_own[...]
    fix_rolled[...] = pltpu.roll(fix, 64, 1)
    fix_got[s] = fix
    to_three_regions(fix_own, fix_rolled, fix_got, 5, 6)

    to_north2.wait_recv()
    to_south2.wait_recv()
    for a in range(NL):
        before = pick(masked(s > 0, got_north2[...]) if a == 0 else comb[a - 1, :, H:2 * H],
                      unsouth[(a + NL - 1) % NL])
        after = pick(masked(s < S - 1, got_south2[...]) if a == NL - 1 else comb[a + 1, :, 0:H],
                     south[a:a + 1, :])
        to_east2(a).wait_recv()
        to_west2(a).wait_recv()
        west = masked(b > 0, pick(got_west2[a], unwest[a]))
        east_side = masked(b < R - 1, pick(got_east2[a], east[a:a + 1, :]))
        fixed[:, 4 * H * a:4 * H * (a + 1)] = comb[a] + jnp.concatenate(
            [before, after, west, east_side], axis=1)

    arrived(lift_got, 3 * S - 1, step_recv.at[4])
    for j in range(3):
        for g in range(S):
            two[G * g:G * (g + 1), j * N2:(j + 1) * N2] = lift_got[j * S + g]
    two_both = jnp.concatenate(split(two[...]), axis=0)
    for a in range(NL):
        e = nn(two_both, looks[a])
        at = 4 * H * a
        fixed[:, at:at + 4 * H] += three(nn, e[:K] + e[K:], big_b_high[a], big_b_low[a])

    arrived(fix_got, S - 1, step_recv.at[5])
    for g in range(S):
        tf[G * g:G * (g + 1), 0:H] = fix_got[g]
    f_high, f_low = split(tf[:, 0:H])
    f_both = jnp.concatenate([f_high, f_low], axis=0)
    for a in range(NL):
        both = nn(f_both, big_q_high[a, 0:H, :])
        value = fixed[:, 4 * H * a:4 * H * (a + 1)] + both[:K] + both[K:] + nn(
            f_high, big_q_low[a, 0:H, :])
        out[a, 0, :, 0:2 * H] = value[:, 0:2 * H]
        fixed[:, 4 * H * a + 2 * H:4 * H * (a + 1)] = value[:, 2 * H:]

    arrived(fix_got, 2 * S, step_recv.at[6])
    for g in range(S):
        tf[G * g:G * (g + 1), 0:H] = fix_got[S + g]
        tf[G * g:G * (g + 1), H:2 * H] = fix_got[2 * S + g]
    f_high, f_low = split(tf[...])
    f_both = jnp.concatenate([f_high, f_low], axis=0)
    for a in range(NL):
        both = nn(f_both, big_q_high[a, :, 2 * H:])
        out[a, 0, :, 2 * H:] = fixed[:, 4 * H * a + 2 * H:4 * H * (a + 1)] + both[:K] + both[
            K:] + nn(f_high, big_q_low[a, :, 2 * H:])

    for first in ((to_west, to_east, to_north, to_south),
                  (to_west2, to_east2, to_north2, to_south2)):
        for a in range(NL):
            first[0](a).wait_send()
            first[1](a).wait_send()
        first[2].wait_send()
        first[3].wait_send()
    for copy in more:
        copy.wait_send()
    table_east.wait_send()
    table_south.wait_send()
    arrived(top_got, S - 1, step_send.at[0])
    arrived(rows_got, S - 1, step_send.at[1])
    arrived(cast_got, R - 1, step_send.at[2])
    arrived(l2inv, (S - 1) * OWN, step_send.at[3])
    arrived(lift_got, 3 * S - 1, step_send.at[4])
    arrived(fix_got, S - 1, step_send.at[5])
    arrived(fix_got, 2 * S, step_send.at[6])


def solution(mesh):
    S, R = mesh.shape["sub"], mesh.shape["region"]

    def on_device(*args):
        NL, _, K, B = args[0].shape
        C1 = args[2].shape[2]
        P2, N2 = args[8].shape[1:]
        NA = args[6].shape[0]
        G = K // S
        vm = pltpu.VMEM
        edge = [vm((NL, K, H), F32), vm((NL, K, H), F32), vm((K, H), F32), vm((K, H), F32)]
        scratch = [
            vm((NL, K, B), F32), vm((NL, B, B), F32), vm((NL, C1, B), F32),
            vm((NL, H), jnp.int32), vm((NL, H), jnp.int32), vm((1, H), jnp.int32),
            vm((NL, H), jnp.int32), vm((NL, C1), jnp.int32), vm((R, NA), jnp.int32), vm((N2, N2), F32), vm((P2, N2), F32), vm((64, N2), F32),
            vm((P2, R * P2), F32), vm((R * P2 + 8, P2), F32), vm((NL, B), F32),
            vm((NL, K, H), jnp.int32), vm((NL, K, H), jnp.int32),
            vm((NL, N2, C1), BF16), vm((128, NL * B), BF16), vm((128, NL * B), BF16),
            vm((128, N2), BF16), vm((64 * R, P2), BF16), vm((64 * R, P2), BF16),
            *edge,
            vm((K, NL * B), F32), vm((K, NL * B), F32),
            vm((2 * G, N2), F32),
            vm((S, G, N2), F32), vm((S, G, N2), F32), vm((G, N2), F32), vm((3 * S, G, N2), F32),
            vm((S, G, H), F32), vm((S, G, H), F32), vm((G, H), F32), vm((R, G, H), F32),
            vm((2 * G, R // 2 * H), F32), vm((G, H), F32), vm((3 * S, G, H), F32),
            vm((K, 3 * N2), F32), vm((K, 2 * H), F32),
            vm((NL, K, B), F32), *edge,
            vm((NL, B), F32), vm((NL, C1, H), F32), vm((NL, C1, H), F32), vm((C1, H), F32),
            vm((C1, H), F32), vm((NL, C1), jnp.int32), vm((NL, C1), jnp.int32),
            vm((1, C1), jnp.int32), vm((1, C1), jnp.int32), vm((P2, N2), F32), vm((P2, N2), F32),
            vm((NL, H), jnp.int32), vm((NL, 3 * N2, H), BF16),
            vm((NL, H, B), BF16), vm((NL, H, B), BF16),
            vm((NL, 256, B), BF16), vm((NL, 256, B), BF16), vm((G, H), F32),
            pltpu.SemaphoreType.REGULAR((5,)),
            pltpu.SemaphoreType.DMA((10,)), pltpu.SemaphoreType.DMA((10,)),
            pltpu.SemaphoreType.DMA((10,)),
            pltpu.SemaphoreType.DMA((2, 2, NL)), pltpu.SemaphoreType.DMA((2, 2, NL)),
            pltpu.SemaphoreType.DMA((2, 4)), pltpu.SemaphoreType.DMA((2, 4)),
            pltpu.SemaphoreType.DMA((7,)), pltpu.SemaphoreType.DMA((7,)),
        ]
        return pl.pallas_call(
            functools.partial(kernel, S, R, NL, K, C1, P2, N2),
            out_shape=jax.ShapeDtypeStruct(args[0].shape, F32),
            in_specs=[pl.BlockSpec(memory_space=pl.ANY)] * len(args),
            out_specs=pl.BlockSpec(memory_space=pltpu.VMEM),
            scratch_shapes=scratch,
            compiler_params=pltpu.CompilerParams(
                collective_id=0, has_side_effects=True, vmem_limit_bytes=56 * 2**20),
        )(*args[:6], args[6].T, args[7], jnp.transpose(args[8], (1, 0, 2)), args[9].T)

    in_specs = (
        P("sub", "region", None, None),
        P("sub", "region", None, None),
        P("sub", "region", None, None),
        P("sub", "region", None),
        P("sub", "region", None),
        P("sub", "region", None),
        P(),
        P("region", "sub", None),
        P("region", None, None),
        P(None, "region"),
    )
    out_specs = P("sub", "region", None, None)
    return jax.shard_map(
        on_device, mesh=mesh, in_specs=in_specs, out_specs=out_specs, check_vma=False
    )
```

```python
import functools

import jax
import jax.numpy as jnp
from jax import lax
from jax.experimental import pallas as pl
from jax.experimental.pallas import tpu as pltpu
from jax.sharding import PartitionSpec as P

H = 128
EARLY = 2
X = 4
MESH = pl.DeviceIdType.MESH
F32 = jnp.float32
BF16 = jnp.bfloat16


def split(x):
    high = x.astype(BF16)
    return high, (x - high.astype(F32)).astype(BF16)


def nn(a, b):
    return jnp.dot(a, b, preferred_element_type=F32)


def nt(a, b):
    return lax.dot_general(a, b, (((1,), (1,)), ((), ())), preferred_element_type=F32)


def three(product, x, high, low):
    rows = x.shape[0]
    x_high, x_low = split(x)
    both = product(jnp.concatenate([x_high, x_low], axis=0), high)
    return both[:rows] + both[rows:] + product(x_high, low)


def pick(face, order):
    return jnp.take_along_axis(face, jnp.broadcast_to(order, face.shape), axis=1)


def kernel(
    S, R, NL, K, C1, P2, N2,
    pieces, local_inverse, basis, match_south, match_east, primal_index, stiffness,
    level2_inverse, level2_basis, top_inverse,
    out,
    pc, inv, bas, south, east, north_table, west_table, index, stiff, l2inv, l2b, l2pad, topt, topv,
    weight, unsouth, unwest,
    look, lbb_high, lbb_low, lb_stack, t_high, t_low,
    got_west, got_east, got_north, got_south,
    asm, fixed, lhs_two, rows_sent, rows_got, lift_own, lift_got,
    top_sent, top_got, cast_own, cast_got, lhs, fix_own, fix_got, two, tf,
    comb, got_west2, got_east2, got_north2, got_south2,
    weight_near, bas_west, bas_east, bas_north, bas_south, index_west, index_east, index_north,
    index_south, l2_west, l2_east, slots, looks, big_b_high, big_b_low, big_q_high, big_q_low,
    fix_rolled, relay, more_send, more_recv,
    load_sem, edge_send, edge_recv, small_send, small_recv, step_send, step_recv,
):
    s = lax.axis_index("sub")
    b = lax.axis_index("region")
    G = K // S
    OWN = N2 // S
    north_of, south_of = (lax.rem(s + S - 1, S), b), (lax.rem(s + 1, S), b)
    west_of, east_of = (s, lax.rem(b + R - 1, R)), (s, lax.rem(b + 1, R))

    barrier = pltpu.get_barrier_semaphore()

    def tell(region, own=s):
        pl.semaphore_signal(barrier, inc=1, device_id=(own, region), device_id_type=MESH)

    def tell_sub(i, c):
        tell(b, lax.rem(s + i, S))
        return c

    up, down = lax.rem(b + X, R), lax.rem(b + R - X, R)

    def relay_start(k, regions):
        for region in regions:
            pl.semaphore_signal(
                relay.at[k], inc=1, device_id=(s, region), device_id_type=MESH)

    def relay_wait(k):
        pl.semaphore_wait(relay.at[k], 2)

    own_rows = pl.ds(pl.multiple_of(s * OWN, 8), OWN)
    loads = [
        pltpu.make_async_copy(match_east.at[:, 0], east, load_sem.at[0]),
        pltpu.make_async_copy(match_south.at[:, 0], south, load_sem.at[1]),
        pltpu.make_async_copy(pieces.at[:, 0], pc, load_sem.at[2]),
        pltpu.make_async_copy(stiffness, stiff, load_sem.at[3]),
        pltpu.make_async_copy(primal_index.at[:, 0], index, load_sem.at[4]),
        pltpu.make_async_copy(basis.at[:, 0], bas, load_sem.at[5]),
        pltpu.make_async_copy(level2_basis.at[:, 0], l2b, load_sem.at[6]),
        pltpu.make_async_copy(level2_inverse.at[0], l2inv.at[own_rows], load_sem.at[7]),
        pltpu.make_async_copy(top_inverse, topt, load_sem.at[8]),
        pltpu.make_async_copy(local_inverse.at[:, 0], inv, load_sem.at[9]),
    ]
    for region in (east_of[1], west_of[1], up, down):
        tell(region)
    for i in range(1, X):
        tell(b // X * X + lax.rem(b + i, X))
    lax.fori_loop(1, S, tell_sub, 0)
    for load in loads:
        load.start()
    pl.semaphore_wait(barrier, 4 + X - 1 + S - 1)
    relay_start(0, (up, down))
    relay_start(4, (east_of[1], west_of[1]))

    def remote(src, dst, send, recv, device):
        return pltpu.make_async_remote_copy(
            src_ref=src, dst_ref=dst, send_sem=send, recv_sem=recv, device_id=device,
            device_id_type=MESH)

    def edges(phase, face, west_got, east_got, north_got, south_got):
        def to_west(a):
            return remote(face(a, 2), east_got.at[a],
                          edge_send.at[phase, 0, a], edge_recv.at[phase, 0, a], west_of)

        def to_east(a):
            return remote(face(a, 3), west_got.at[a],
                          edge_send.at[phase, 1, a], edge_recv.at[phase, 1, a], east_of)

        to_north = remote(face(0, 0), south_got,
                          small_send.at[phase, 0], small_recv.at[phase, 0], north_of)
        to_south = remote(face(NL - 1, 1), north_got,
                          small_send.at[phase, 1], small_recv.at[phase, 1], south_of)
        return to_west, to_east, to_north, to_south

    to_west, to_east, to_north, to_south = edges(
        0, lambda a, f: pieces.at[a, 0, :, pl.ds(f * H, H)],
        got_west, got_east, got_north, got_south)
    table_east = remote(match_east.at[:, 0], west_table,
                        small_send.at[0, 2], small_recv.at[0, 2], east_of)
    table_south = remote(match_south.at[NL - 1], north_table,
                         small_send.at[0, 3], small_recv.at[0, 3], south_of)
    table_east.start()
    table_south.start()
    for a in range(NL):
        to_west(a).start()
        to_east(a).start()
    to_north.start()
    to_south.start()

    def others(count, me, make):
        for i in sorted(range(1, count), key=lambda i: (abs(count // 2 - i), i)):
            make(lax.rem(me + i, count)).start()

    others(S, s, lambda o: remote(
        level2_inverse.at[0], l2inv.at[own_rows], step_send.at[3], step_recv.at[3], (o, b)))

    def face(f):
        return basis.at[:, 0, :, pl.ds(f * H, H)]

    more = [(face(3), bas_west, east_of), (primal_index.at[:, 0], index_west, east_of),
            (level2_basis.at[:, 0], l2_west, east_of),
            (face(2), bas_east, west_of), (primal_index.at[:, 0], index_east, west_of),
            (level2_basis.at[:, 0], l2_east, west_of),
            (basis.at[NL - 1, 0, :, pl.ds(H, H)], bas_north, south_of),
            (primal_index.at[NL - 1], index_north, south_of),
            (basis.at[0, 0, :, pl.ds(0, H)], bas_south, north_of),
            (primal_index.at[0], index_south, north_of)]
    more = [remote(src, dst, more_send.at[i], more_recv.at[i], device)
            for i, (src, dst, device) in enumerate(more)]
    for copy in more:
        copy.start()

    lane = lax.broadcasted_iota(jnp.int32, (K, H), 1).astype(F32).astype(BF16)
    face_row = lax.broadcasted_iota(jnp.int32, (H, H), 0)

    def invert(order):
        hit = (face_row == order).astype(F32).astype(BF16)
        return nt(lane, hit).astype(jnp.int32)

    loads[0].wait()
    loads[1].wait()
    for a in range(NL - 1):
        unsouth[a] = invert(south[a:a + 1, :])

    relay_wait(0)
    relay_start(1, (up, down))

    loads[3].wait()
    levels = stiff[...].astype(F32)
    regions = lax.broadcasted_iota(jnp.int32, levels.shape, 0)
    spots = (lax.broadcasted_iota(jnp.int32, (NL, levels.shape[1]), 1)
             - lax.broadcasted_iota(jnp.int32, (NL, levels.shape[1]), 0) - s * NL)

    def level(region, step):
        row = jnp.sum(jnp.where(regions == region, levels, 0.0), axis=0, keepdims=True)
        return jnp.sum(jnp.where(spots == step, row, 0.0), axis=1, keepdims=True)

    own = level(b, 0)
    for f, other in enumerate((level(b, -1), level(b, 1), level(b - 1, 0), level(b + 1, 0))):
        weight[:, f * H:(f + 1) * H] = jnp.broadcast_to(own / (own + other), (NL, H))
        weight_near[:, f * H:(f + 1) * H] = jnp.broadcast_to(other / (own + other), (NL, H))

    loads[4].wait()
    loads[5].wait()
    loads[6].wait()
    l2pad[...] = jnp.zeros_like(l2pad)
    l2pad[0:P2, :] = l2b[...]
    l2_high, l2_low = split(l2pad[...])
    lb_stack[0:64, :] = l2_high
    lb_stack[64:128, :] = l2_low
    unknown = lax.broadcasted_iota(jnp.int32, (N2, C1), 0)
    odd = lax.rem(b, 2)
    lbb_high[...] = jnp.zeros_like(lbb_high)
    lbb_low[...] = jnp.zeros_like(lbb_low)
    half = pl.ds(pl.multiple_of(odd * 64, 64), 64)
    for a in range(NL):
        hit = (unknown == index[a:a + 1, :]).astype(F32).astype(BF16)
        look[a] = hit
        lb = nn(lb_stack[...], hit)
        lb_high, lb_low = lb[:64].astype(BF16), lb[64:].astype(BF16)
        b_high, b_low = split(bas[a])
        both = nn(jnp.concatenate([lb_high, lb_low], axis=0), b_high)
        lbb = (both[:64] + both[64:] + nn(lb_high, b_low)) * weight[a:a + 1, :]
        high, low = split(lbb)
        lbb_high[half, 4 * H * a:4 * H * (a + 1)] = high
        lbb_low[half, 4 * H * a:4 * H * (a + 1)] = low

    relay_wait(1)
    relay_start(2, (up, down))

    loads[8].wait()
    for c in range(R * P2 // 128):
        topv[128 * c:128 * (c + 1), :] = topt[:, 128 * c:128 * (c + 1)].T
    topv[R * P2:, :] = jnp.zeros_like(topv[R * P2:, :])

    def spread_top(p, c):
        block = topv[pl.ds(pl.multiple_of(2 * P2 * p, 8), 2 * P2 + 8), :]
        pair = jnp.concatenate([block[0:64], block[P2:P2 + 64]], axis=0)
        high, low = split(pair)
        at = pl.ds(pl.multiple_of(128 * p, 128), 128)
        t_high[at, :] = high
        t_low[at, :] = low
        return c

    lax.fori_loop(0, R // 2, spread_top, 0)

    def masked(condition, value):
        return jnp.where(condition, value, jnp.zeros_like(value))

    relay_wait(2)
    relay_start(3, (up, down))

    table_south.wait_recv()
    unsouth[NL - 1] = invert(north_table[...])
    table_east.wait_recv()
    for a in range(NL):
        unwest[a] = invert(west_table[a:a + 1, :])
    loads[2].wait()
    to_north.wait_recv()
    to_south.wait_recv()
    for a in range(NL):
        before = pick(masked(s > 0, got_north[...]) if a == 0 else pc[a - 1, :, H:2 * H],
                      unsouth[(a + NL - 1) % NL])
        after = pick(masked(s < S - 1, got_south[...]) if a == NL - 1 else pc[a + 1, :, 0:H],
                     south[a:a + 1, :])
        at = 4 * H * a
        asm[:, at:at + H] = pc[a, :, 0:H] + before
        asm[:, at + H:at + 2 * H] = pc[a, :, H:2 * H] + after
    top = jnp.zeros((K, H), F32)
    for a in range(NL):
        at = 4 * H * a
        to_east(a).wait_recv()
        asm[:, at + 2 * H:at + 3 * H] = pc[a, :, 2 * H:3 * H] + masked(
            b > 0, pick(got_west[a], unwest[a]))
        to_west(a).wait_recv()
        asm[:, at + 3 * H:at + 4 * H] = pc[a, :, 3 * H:] + masked(
            b < R - 1, pick(got_east[a], east[a:a + 1, :]))
        top += three(nt, asm[:, at:at + 4 * H], lbb_high[:, at:at + 4 * H],
                     lbb_low[:, at:at + 4 * H])

    for g in range(S):
        top_sent[g] = top[G * g:G * (g + 1)]

    def arrived(ref, count, sem):
        pltpu.make_async_copy(ref.at[pl.ds(0, count)], ref.at[pl.ds(0, count)], sem).wait()

    top_got[s] = top_sent[s]
    others(S, s, lambda o: remote(
        top_sent.at[o], top_got.at[s], step_send.at[0], step_recv.at[0], (o, b)))

    two_in = jnp.zeros((K, N2), F32)
    for a in range(NL):
        scaled = asm[:, 4 * H * a:4 * H * (a + 1)] * weight[a:a + 1, :]
        asm[:, 4 * H * a:4 * H * (a + 1)] = scaled
        b_high, b_low = split(bas[a])
        c_high, c_low = split(three(nt, scaled, b_high, b_low))
        both = nt(jnp.concatenate([c_high, c_low], axis=0), look[a])
        two_in += both[:K] + both[K:]
    for g in range(S):
        rows_sent[g] = two_in[G * g:G * (g + 1)]
    rows_got[s] = rows_sent[s]
    others(S, s, lambda o: remote(
        rows_sent.at[o], rows_got.at[s], step_send.at[1], step_recv.at[1], (o, b)))

    to_west2, to_east2, to_north2, to_south2 = edges(
        1, lambda a, f: comb.at[a, :, pl.ds(f * H, H)],
        got_west2, got_east2, got_north2, got_south2)
    loads[9].wait()

    def solve(a, c):
        high, low = split(inv[a])
        at = pl.ds(pl.multiple_of(4 * H * a, 4 * H), 4 * H)
        comb[a] = three(nn, asm[:, at], high, low) * weight[pl.ds(a, 1), :]
        to_west2(a).start()
        to_east2(a).start()
        return c

    lax.fori_loop(0, EARLY, solve, 0)

    arrived(top_got, S - 1, step_recv.at[0])
    mine = top_got[0]
    for g in range(1, S):
        mine += top_got[g]
    cast_own[...] = mine
    cast_got[b] = mine

    relay_wait(3)

    def cast(i, c):
        o = lax.rem(b + i, R)
        remote(cast_own, cast_got.at[b], step_send.at[2], step_recv.at[2], (s, o)).start()
        return c

    for i in sorted(range(1, R), key=lambda i: (abs(R // 2 - i), i)):
        cast(i, 0)

    lax.fori_loop(EARLY, NL, solve, 0)
    to_north2.start()
    to_south2.start()

    loads[7].wait()
    arrived(l2inv, (S - 1) * OWN, step_recv.at[3])
    i_high, i_low = split(l2inv[...])
    arrived(rows_got, S - 1, step_recv.at[1])
    two_mine = rows_got[0]
    for g in range(1, S):
        two_mine += rows_got[g]
    high = two_mine.astype(BF16).astype(F32)
    lhs_two[0:G, :] = high
    lhs_two[G:2 * G, :] = two_mine - high
    left = lhs_two[...].astype(BF16)
    first = nn(left, i_high)
    lift4 = first[0:G] + first[G:2 * G] + nn(left, i_low)[0:G]
    relay_wait(4)
    lift_own[...] = lift4
    lift_got[s] = lift4

    def spread(i, src, rolled, got, k):
        o = lax.rem(s + i, S)
        remote(rolled, got.at[S + s], step_send.at[k], step_recv.at[k], (o, east_of[1])).start()
        remote(src, got.at[2 * S + s], step_send.at[k], step_recv.at[k], (o, west_of[1])).start()

    def to_three_regions(src, rolled, got, k, k_near):
        def body(i, c):
            spread(i, src, rolled, got, k_near)
            o = lax.rem(s + i, S)
            remote(src, got.at[s], step_send.at[k], step_recv.at[k], (o, b)).start()
            return c
        for i in sorted(range(1, S), key=lambda i: (abs(S // 2 - i), i)):
            body(i, 0)
        spread(0, src, rolled, got, k_near)

    to_three_regions(lift_own, lift_own, lift_got, 4, 4)

    for copy in more:
        copy.wait_recv()
    slots[...] = jnp.full_like(slots, -1)
    slots[:, 0:C1] = index[...]
    slots[0:1, C1:2 * C1] = index_north[...]
    slots[1:NL, C1:2 * C1] = index[0:NL - 1, :]
    slots[0:NL - 1, 2 * C1:3 * C1] = index[1:NL, :]
    slots[NL - 1:NL, 2 * C1:3 * C1] = index_south[...]
    slots[:, 3 * C1:4 * C1] = index_west[...]
    slots[:, 4 * C1:5 * C1] = index_east[...]
    stacks = [lb_stack[...]]
    for level2 in (l2_west, l2_east):
        l2pad[0:P2, :] = level2[...]
        stacks.append(jnp.concatenate(split(l2pad[...]), axis=0))
    spot = lax.broadcasted_iota(jnp.int32, (N2, H), 1)
    unknown = lax.broadcasted_iota(jnp.int32, (N2, H), 0)
    big_q_high[:, 192:256, :] = jnp.zeros_like(big_q_high[:, 192:256, :])
    big_q_low[:, 192:256, :] = jnp.zeros_like(big_q_low[:, 192:256, :])
    gap = jnp.zeros((C1, H), F32)
    for a in range(NL):
        hit = jnp.where(unknown == slots[a:a + 1, :], 1.0, 0.0)
        lb_high, lb_low = [], []
        for j, (low_end, high_end) in enumerate(((0, 3), (3, 4), (4, 5))):
            own_hit = jnp.where((spot >= low_end * C1) & (spot < high_end * C1), hit, 0.0).astype(BF16)
            looks[a, j * N2:(j + 1) * N2, :] = own_hit
            lb = nn(stacks[j], own_hit)
            lb_high.append(lb[0:64])
            lb_low.append(lb[64:128])
        north = bas_north[...] if a == 0 else bas[a - 1, :, H:2 * H]
        north_weight = weight_near[0:1, 0:H] if a == 0 else weight[a - 1:a, H:2 * H]
        after = bas_south[...] if a == NL - 1 else bas[a + 1, :, 0:H]
        after_weight = (weight_near[a:a + 1, H:2 * H] if a == NL - 1
                        else weight[a + 1:a + 2, 0:H])
        faces = [
            pick(north, unsouth[(a + NL - 1) % NL, 0:1, :]) * north_weight,
            pick(after, south[a:a + 1, :]) * after_weight,
            pick(bas_west[a], unwest[a, 0:1, :]) * weight_near[a:a + 1, 2 * H:3 * H],
            pick(bas_east[a], east[a:a + 1, :]) * weight_near[a:a + 1, 3 * H:]]
        rows = [bas[a] * weight[a:a + 1, :]]
        for f in range(4):
            rows.append(jnp.concatenate([gap] * f + [faces[f]] + [gap] * (3 - f), axis=1))
        rows.append(jnp.zeros((H - 5 * C1, 4 * H), F32))
        high, low = split(jnp.concatenate(rows, axis=0))
        big_b_high[a] = high
        big_b_low[a] = low
        q_high = jnp.concatenate(lb_high, axis=0).astype(BF16)
        q_low = jnp.concatenate(lb_low, axis=0).astype(BF16)
        both = nn(jnp.concatenate([q_high, q_low], axis=0), high)
        q_high, q_low = split(both[0:192] + both[192:] + nn(q_high, low))
        big_q_high[a, 0:192, :] = q_high
        big_q_low[a, 0:192, :] = q_low

    arrived(cast_got, R - 1, step_recv.at[2])
    for p in range(R // 2):
        pair = cast_got[2 * p] + cast_got[2 * p + 1]
        high = pair.astype(BF16).astype(F32)
        lhs[0:G, H * p:H * (p + 1)] = high
        lhs[G:2 * G, H * p:H * (p + 1)] = pair - high
    left = lhs[...].astype(BF16)
    first = nn(left, t_high[...])
    fix = first[0:G] + first[G:2 * G] + nn(left, t_low[...])[0:G]
    fix_own[...] = jnp.zeros_like(fix_own)
    fix_own[:, 0:P2] = fix
    fix = fix_own[...]
    fix_rolled[...] = pltpu.roll(fix, 64, 1)
    fix_got[s] = fix
    to_three_regions(fix_own, fix_rolled, fix_got, 5, 6)

    to_north2.wait_recv()
    to_south2.wait_recv()
    for a in range(NL):
        before = pick(masked(s > 0, got_north2[...]) if a == 0 else comb[a - 1, :, H:2 * H],
                      unsouth[(a + NL - 1) % NL])
        after = pick(masked(s < S - 1, got_south2[...]) if a == NL - 1 else comb[a + 1, :, 0:H],
                     south[a:a + 1, :])
        to_east2(a).wait_recv()
        to_west2(a).wait_recv()
        west = masked(b > 0, pick(got_west2[a], unwest[a]))
        east_side = masked(b < R - 1, pick(got_east2[a], east[a:a + 1, :]))
        fixed[:, 4 * H * a:4 * H * (a + 1)] = comb[a] + jnp.concatenate(
            [before, after, west, east_side], axis=1)

    arrived(lift_got, 3 * S - 1, step_recv.at[4])
    for j in range(3):
        for g in range(S):
            two[G * g:G * (g + 1), j * N2:(j + 1) * N2] = lift_got[j * S + g]
    two_both = jnp.concatenate(split(two[...]), axis=0)
    for a in range(NL):
        e = nn(two_both, looks[a])
        at = 4 * H * a
        fixed[:, at:at + 4 * H] += three(nn, e[:K] + e[K:], big_b_high[a], big_b_low[a])

    arrived(fix_got, S - 1, step_recv.at[5])
    for g in range(S):
        tf[G * g:G * (g + 1), 0:H] = fix_got[g]
    f_high, f_low = split(tf[:, 0:H])
    f_both = jnp.concatenate([f_high, f_low], axis=0)
    for a in range(NL):
        both = nn(f_both, big_q_high[a, 0:H, :])
        value = fixed[:, 4 * H * a:4 * H * (a + 1)] + both[:K] + both[K:] + nn(
            f_high, big_q_low[a, 0:H, :])
        out[a, 0, :, 0:2 * H] = value[:, 0:2 * H]
        fixed[:, 4 * H * a + 2 * H:4 * H * (a + 1)] = value[:, 2 * H:]

    arrived(fix_got, 2 * S, step_recv.at[6])
    for g in range(S):
        tf[G * g:G * (g + 1), 0:H] = fix_got[S + g]
        tf[G * g:G * (g + 1), H:2 * H] = fix_got[2 * S + g]
    f_high, f_low = split(tf[...])
    f_both = jnp.concatenate([f_high, f_low], axis=0)
    for a in range(NL):
        both = nn(f_both, big_q_high[a, :, 2 * H:])
        out[a, 0, :, 2 * H:] = fixed[:, 4 * H * a + 2 * H:4 * H * (a + 1)] + both[:K] + both[
            K:] + nn(f_high, big_q_low[a, :, 2 * H:])

    for first in ((to_west, to_east, to_north, to_south),
                  (to_west2, to_east2, to_north2, to_south2)):
        for a in range(NL):
            first[0](a).wait_send()
            first[1](a).wait_send()
        first[2].wait_send()
        first[3].wait_send()
    for copy in more:
        copy.wait_send()
    table_east.wait_send()
    table_south.wait_send()
    arrived(top_got, S - 1, step_send.at[0])
    arrived(rows_got, S - 1, step_send.at[1])
    arrived(cast_got, R - 1, step_send.at[2])
    arrived(l2inv, (S - 1) * OWN, step_send.at[3])
    arrived(lift_got, 3 * S - 1, step_send.at[4])
    arrived(fix_got, S - 1, step_send.at[5])
    arrived(fix_got, 2 * S, step_send.at[6])


def solution(mesh):
    S, R = mesh.shape["sub"], mesh.shape["region"]

    def on_device(*args):
        NL, _, K, B = args[0].shape
        C1 = args[2].shape[2]
        P2, N2 = args[8].shape[1:]
        NA = args[6].shape[0]
        G = K // S
        vm = pltpu.VMEM
        edge = [vm((NL, K, H), F32), vm((NL, K, H), F32), vm((K, H), F32), vm((K, H), F32)]
        scratch = [
            vm((NL, K, B), F32), vm((NL, B, B), F32), vm((NL, C1, B), F32),
            vm((NL, H), jnp.int32), vm((NL, H), jnp.int32), vm((1, H), jnp.int32),
            vm((NL, H), jnp.int32), vm((NL, C1), jnp.int32), vm((R, NA), jnp.int32), vm((N2, N2), F32), vm((P2, N2), F32), vm((64, N2), F32),
            vm((P2, R * P2), F32), vm((R * P2 + 8, P2), F32), vm((NL, B), F32),
            vm((NL, K, H), jnp.int32), vm((NL, K, H), jnp.int32),
            vm((NL, N2, C1), BF16), vm((128, NL * B), BF16), vm((128, NL * B), BF16),
            vm((128, N2), BF16), vm((64 * R, P2), BF16), vm((64 * R, P2), BF16),
            *edge,
            vm((K, NL * B), F32), vm((K, NL * B), F32),
            vm((2 * G, N2), F32),
            vm((S, G, N2), F32), vm((S, G, N2), F32), vm((G, N2), F32), vm((3 * S, G, N2), F32),
            vm((S, G, H), F32), vm((S, G, H), F32), vm((G, H), F32), vm((R, G, H), F32),
            vm((2 * G, R // 2 * H), F32), vm((G, H), F32), vm((3 * S, G, H), F32),
            vm((K, 3 * N2), F32), vm((K, 2 * H), F32),
            vm((NL, K, B), F32), *edge,
            vm((NL, B), F32), vm((NL, C1, H), F32), vm((NL, C1, H), F32), vm((C1, H), F32),
            vm((C1, H), F32), vm((NL, C1), jnp.int32), vm((NL, C1), jnp.int32),
            vm((1, C1), jnp.int32), vm((1, C1), jnp.int32), vm((P2, N2), F32), vm((P2, N2), F32),
            vm((NL, H), jnp.int32), vm((NL, 3 * N2, H), BF16),
            vm((NL, H, B), BF16), vm((NL, H, B), BF16),
            vm((NL, 256, B), BF16), vm((NL, 256, B), BF16), vm((G, H), F32),
            pltpu.SemaphoreType.REGULAR((5,)),
            pltpu.SemaphoreType.DMA((10,)), pltpu.SemaphoreType.DMA((10,)),
            pltpu.SemaphoreType.DMA((10,)),
            pltpu.SemaphoreType.DMA((2, 2, NL)), pltpu.SemaphoreType.DMA((2, 2, NL)),
            pltpu.SemaphoreType.DMA((2, 4)), pltpu.SemaphoreType.DMA((2, 4)),
            pltpu.SemaphoreType.DMA((7,)), pltpu.SemaphoreType.DMA((7,)),
        ]
        return pl.pallas_call(
            functools.partial(kernel, S, R, NL, K, C1, P2, N2),
            out_shape=jax.ShapeDtypeStruct(args[0].shape, F32),
            in_specs=[pl.BlockSpec(memory_space=pl.ANY)] * len(args),
            out_specs=pl.BlockSpec(memory_space=pltpu.VMEM),
            scratch_shapes=scratch,
            compiler_params=pltpu.CompilerParams(
                collective_id=0, has_side_effects=True, vmem_limit_bytes=56 * 2**20),
        )(*args[:6], args[6].T, args[7], jnp.transpose(args[8], (1, 0, 2)), args[9].T)

    in_specs = (
        P("sub", "region", None, None),
        P("sub", "region", None, None),
        P("sub", "region", None, None),
        P("sub", "region", None),
        P("sub", "region", None),
        P("sub", "region", None),
        P(),
        P("region", "sub", None),
        P("region", None, None),
        P(None, "region"),
    )
    out_specs = P("sub", "region", None, None)
    return jax.shard_map(
        on_device, mesh=mesh, in_specs=in_specs, out_specs=out_specs, check_vma=False
    )
```
